256 devices in a mesh: gx: 8 (over z), gy: 32 (over y, x, core).
Axes of the slice: x: 4, y: 4, z: 8, core: 2. Of those that a mesh axis runs over, the one named last changes fastest.
Arguments:
- adjoint_rhs: float32 [2, 3, 8, 2048, 128], P(None, None, 'gx', 'gy'), may hold values from -6 to 6
- block_inverse: float32 [3, 3, 8, 2048, 128], P(None, None, 'gx', 'gy'), may hold values from -0.3 to 1.3, as said below
- x_couplings: float32 [2, 3, 8, 2048, 128], P(None, None, 'gx', 'gy'), may hold values from -0.8 to -0.3
- y_couplings: float32 [2, 3, 8, 2048, 128], P(None, None, 'gx', 'gy'), may hold values from -0.3 to -0.05
- perf_cell: int32 [16384], P(('gx', 'gy')), may hold values from 0 to 8191
- perf_well: int32 [16384], P(('gx', 'gy')), may hold values from 0 to 1023
- perf_weight: float32 [16384], P(('gx', 'gy')), may hold values from 0.5 to 2
- well_adjoint: float32 [3, 1024], P(None, ('gx', 'gy')), may hold values from -6 to 6
Outputs:
- precond: float32 [2, 3, 8, 2048, 128], P(None, None, 'gx', 'gy')
- well_update: float32 [3, 1024], P(None, ('gx', 'gy'))
The draws below stay inside these ranges and needn't reach their ends.
Inputs may be any that keep to these rules, and one draw needn't show every extreme that they name: `perf_cell`: local cell index within the owning device's block. `block_inverse`: diagonal entries are at least 0.5, off-diagonal ones at most 0.3 in magnitude.
All inputs are finite; a program needn't handle non-finite values.
Results may differ from the reference program's by a relative error of at most 0.00017.
Values sent between devices are 32-bit elements; how exact they have to be, the bound alone decides.
No kernel may reach another device: no remote copies, remote signals or barrier semaphores. Data moves between devices by JAX's collectives and lax.ppermute only.
A program may use at most 64 MiB of HBM per device.

```python
import math
import jax
import jax.numpy as jnp
import numpy as np
from jax import lax

NC = 3
PX = 1
CY = 64
CZ = 128
PERF_DEV = 64
NX = 8
NY = 2048
NZ = 128
WELLS = 1024
PERFS = 16384
N_GY = 32


def draw_block_inverse(key, part):
    uniform_values = jax.random.uniform(key, (NC, NC, NX, NY, NZ), jnp.float32)
    diagonal_mask = (jnp.arange(NC)[:, None] == jnp.arange(NC)[None, :])[:, :, None, None, None]
    diagonal = 0.6 + 0.6 * uniform_values
    offdiag = 0.25 * (2.0 * uniform_values - 1.0)
    return jnp.where(diagonal_mask, diagonal, offdiag)


def touch_ends(values, key, smallest, largest):
    place = [jax.random.randint(jax.random.fold_in(key, axis), (), 0, length) for axis, length in enumerate(values.shape)]
    widest = values.shape.index(max(values.shape))
    neighbour = place[:widest] + [(place[widest] + 1) % values.shape[widest]] + place[widest + 1:]
    return values.at[tuple(place)].set(smallest).at[tuple(neighbour)].set(largest)


def shard_levels(stream_key, shape, cuts, smallest, top_value):
    factor_of = 1.0
    for dim, parts in cuts:
        steps = jax.random.uniform(jax.random.fold_in(jax.random.fold_in(stream_key, 6), dim), (parts,), jnp.float32, smallest / len(cuts), top_value / len(cuts))
        factor_of = factor_of * jnp.repeat(jnp.exp(steps), shape[dim] // parts).reshape((-1,) + (1,) * (len(shape) - 1 - dim))
    return factor_of


def rank_bounds(count, lean):
    weights = [(1 << 20) // math.isqrt(grade ** lean) + 1 for grade in range(1, count + 1)]
    spread = 1 + sum(weights) // (1 << 30)
    return np.cumsum(np.array([max(1, weight // spread) for weight in weights]))


def ranked_ids(stream_key, shape, count, lean):
    table = rank_bounds(count, lean)
    pick = jax.random.randint(jax.random.fold_in(stream_key, 1), shape, 0, int(table[count - 1]))
    standing = jnp.searchsorted(jnp.asarray(table, jnp.int32), pick, side="right")
    return jax.random.permutation(jax.random.fold_in(stream_key, 2), count)[standing].astype(jnp.int32)


def noise(key, shape, scale, reach, cuts=(), held_as=jnp.bfloat16):
    values = scale * jax.random.normal(key, shape, jnp.float32)
    if cuts:
        values = values * shard_levels(key, shape, cuts, -0.22, 0.18)
    return jnp.clip(values, -reach, reach).astype(held_as)


def setup_inputs(seed: int = 0) -> dict:
    key_list = jax.random.split(jax.random.key(seed), 9)
    return {
        "adjoint_rhs": noise(key_list[0], (2, NC, NX, NY, NZ), 1.0, 6.0, ((2, 8), (3, 32)), jnp.float32),
        "block_inverse": draw_block_inverse(jax.random.fold_in(key_list[8], 71), 0),
        "x_couplings": jnp.clip(-0.8 + 0.5 * jax.random.uniform(key_list[2], (2, NC, NX, NY, NZ), jnp.float32) ** shard_levels(key_list[2], (2, NC, NX, NY, NZ), ((2, 8), (3, 32)), -0.2, 0.2), -0.8, -0.3),
        "y_couplings": jnp.clip(-0.3 + 0.25 * jax.random.uniform(key_list[3], (2, NC, NX, NY, NZ), jnp.float32) ** shard_levels(key_list[3], (2, NC, NX, NY, NZ), ((2, 8), (3, 32)), -0.2, 0.2), -0.3, -0.05),
        "perf_cell": touch_ends(jax.random.randint(key_list[4], (PERFS,), 0, PX * CY * CZ), jax.random.fold_in(key_list[4], 1), 0, (PX * CY * CZ) - 1).astype(jnp.int32),
        "perf_well": touch_ends(ranked_ids(key_list[5], (PERFS,), WELLS, 2), jax.random.fold_in(key_list[5], 3), 0, WELLS - 1).astype(jnp.int32),
        "perf_weight": jnp.clip(jnp.exp(math.log(2.0) - 1.3862944 * jax.random.uniform(key_list[6], (PERFS,), jnp.float32) ** shard_levels(key_list[6], (PERFS,), ((0, 256),), -0.2, 0.2)), 0.5, 2.0),
        "well_adjoint": noise(key_list[7], (NC, WELLS), 1.0, 6.0, ((1, 256),), jnp.float32),
    }


def apply_inverse(inverse, values):
    return inverse[:, 0] * values[None, 0] + inverse[:, 1] * values[None, 1] + inverse[:, 2] * values[None, 2]


def plane_apply(values, inverse, lower, upper):
    weighted = apply_inverse(inverse, values)
    border = jnp.zeros((weighted.shape[0], 1, weighted.shape[2]), jnp.float32)
    below = jnp.concatenate([border, weighted[:, :-1]], axis=1)
    above = jnp.concatenate([weighted[:, 1:], border], axis=1)
    return apply_inverse(inverse, values - lower * below - upper * above)


def factor_solve(rhs, inverse_t, x_low, x_up, y_low, y_up):
    rhs_t = jnp.moveaxis(rhs, 1, 0)

    def forward(previous, items):
        source, inverse, low, ylo, yup = items
        current = plane_apply(source - low * previous, inverse, ylo, yup)
        return current, current

    start = jnp.zeros(rhs_t.shape[1:], jnp.float32)
    _, forward_planes = lax.scan(forward, start, (rhs_t, inverse_t, x_low, y_low, y_up))

    def backward(following, items):
        current_q, inverse, high, ylo, yup = items
        current = current_q - plane_apply(high * following, inverse, ylo, yup)
        return current, current

    _, result = lax.scan(backward, start, (forward_planes, inverse_t, x_up, y_low, y_up), reverse=True)
    return jnp.moveaxis(result, 0, 1)


def reference(adjoint_rhs, block_inverse, x_couplings, y_couplings, perf_cell, perf_well, perf_weight, well_adjoint):
    device = (jnp.arange(PERFS) // PERF_DEV).astype(jnp.int32)
    block_x = device // N_GY
    block_y = device % N_GY
    plane = perf_cell // (CY * CZ)
    line = (perf_cell // CZ) % CY
    depth = perf_cell % CZ
    flat = ((block_x * PX + plane) * NY + block_y * CY + line) * NZ + depth
    flat = flat.astype(jnp.int32)
    terms = well_adjoint[:, perf_well] * perf_weight[None]
    source = jnp.zeros((NC, NX * NY * NZ), jnp.float32).at[:, flat].add(terms)
    source = source.reshape(NC, NX, NY, NZ)
    inverse_t = jnp.moveaxis(block_inverse, 2, 0)
    x_low = jnp.moveaxis(x_couplings[0], 1, 0)
    x_up = jnp.moveaxis(x_couplings[1], 1, 0)
    y_low = jnp.moveaxis(y_couplings[0], 1, 0)
    y_up = jnp.moveaxis(y_couplings[1], 1, 0)
    first = factor_solve(adjoint_rhs[0] + source, inverse_t, x_low, x_up, y_low, y_up)
    second = factor_solve(adjoint_rhs[1] + source, inverse_t, x_low, x_up, y_low, y_up)
    values = second.reshape(NC, NX * NY * NZ)[:, flat] * perf_weight[None]
    well_update = jax.ops.segment_sum(values.T, perf_well, num_segments=WELLS).T
    return jnp.stack([first, second]), well_update
```

```python
import functools

import jax
import jax.numpy as jnp
from jax import lax
from jax.experimental import pallas as pl
from jax.experimental.pallas import tpu as pltpu
from jax.sharding import PartitionSpec as P

F32 = jnp.float32
BF16 = jnp.bfloat16
PLANES = 8
LINES = 64
ZC = 16
PAIRS = 14
STRIP = 16
VMEM_LIMIT = 24 * 1024 * 1024

VMEM = pl.BlockSpec(memory_space=pltpu.VMEM)
SMEM = pl.BlockSpec(memory_space=pltpu.SMEM)


def split3(x):
    hi = x.astype(BF16).astype(F32)
    rest = x - hi
    mid = rest.astype(BF16).astype(F32)
    lo = rest - mid
    return hi, mid, lo


def split_rows(x):
    return jnp.concatenate(split3(x), axis=0).astype(BF16)


def join_rows(y, rows):
    return y[0:rows] + y[rows : 2 * rows] + y[2 * rows : 3 * rows]


def lane_iota(rows):
    return lax.broadcasted_iota(jnp.int32, (rows, 128), 1)


def row_iota(rows):
    return lax.broadcasted_iota(jnp.int32, (rows, 128), 0)


def roll_lanes(x, shift):
    shift %= 128
    return x if shift == 0 else pltpu.roll(x, shift, 1)


def pack_kernel(me_ref, rhs, einv, xc, yc, *rest):
    outs, turned = rest[:PLANES], rest[PLANES]
    me = me_ref[0]
    arrays = (
        [(rhs, i) for i in range(6)]
        + [(einv, i) for i in range(9)]
        + [(xc, i) for i in range(6)]
        + [(yc, i) for i in range(6)]
    )
    for g in range(PAIRS):
        ref, i = arrays[2 * g]
        top = ref[i]
        if 2 * g + 1 < len(arrays):
            ref, i = arrays[2 * g + 1]
            low = ref[i]
        else:
            low = jnp.zeros((LINES, 128), F32)
        turned[g] = jnp.concatenate([top, low], axis=0).T
    for d in range(PLANES):
        target = (me + d) & 7
        outs[d][...] = turned[:, pl.ds(pl.multiple_of(target * ZC, ZC), ZC), :]


def perf_tiles(zrefs):
    half = lane_iota(8) < 64
    return [
        jnp.where(half, zrefs[2 * j][...], roll_lanes(zrefs[2 * j + 1][...], 64))
        for j in range(PLANES // 2)
    ]


def source_kernel(me_ref, *rest):
    zrefs, (src_ref, pick_ref) = rest[:PLANES], rest[PLANES:]
    me = me_ref[0]
    tiles = perf_tiles(zrefs)
    lane = lane_iota(128)
    row = row_iota(128)
    wells = [t[4:5].astype(jnp.int32) for t in tiles]
    picked = [jnp.zeros((32, 128), F32) for _ in tiles]
    for d in range(PLANES):
        base = ((me - d) & 7) * 128
        values = zrefs[d][...]
        parts = jnp.concatenate(list(split3(values)) + [jnp.zeros((8, 128), F32)], axis=0).astype(BF16)
        for j in range(4):
            hot = jnp.where(wells[j] == row + base, 1.0, 0.0).astype(BF16)
            pick_ref[d, :, 128 * j : 128 * j + 128] = hot
            picked[j] += jnp.dot(parts, hot, preferred_element_type=F32)
    half = lane_iota(1) < 64
    depth_row = row_iota(ZC)
    low = lane_iota(ZC) < 64
    for j in range(4):
        term = join_rows(picked[j], 8)[0:3] * tiles[j][5:6]
        cell = tiles[j][3:4].astype(jnp.int32)
        at_z = (cell & 127) == depth_row + me * ZC
        at_y = jnp.where(((cell >> 7) & 63) == row, 1.0, 0.0).astype(BF16)
        rows = []
        for side in range(2):
            keep = jnp.logical_and(at_z, half if side == 0 else jnp.logical_not(half))
            rows += [jnp.where(keep, term[c : c + 1], 0.0) for c in range(3)]
        left = split_rows(jnp.concatenate(rows, axis=0))
        spread = lax.dot_general(left, at_y, (((1,), (1,)), ((), ())), preferred_element_type=F32)
        spread = join_rows(spread, 96)
        for side in range(2):
            c0, c1, c2 = (spread[48 * side + 16 * c : 48 * side + 16 * c + 16] for c in range(3))
            d = 2 * j + side
            src_ref[d, 0] = jnp.where(low, c0, roll_lanes(c1, 64))
            src_ref[d, 1] = jnp.where(low, c2, roll_lanes(c0, 64))
            src_ref[d, 2] = jnp.where(low, c1, roll_lanes(c2, 64))


def strip_kernel(*rest):
    chunks, src, (first_ref, last_ref) = rest[:PLANES], rest[PLANES], rest[PLANES + 1 :]
    slot = (lane_iota(ZC) & 63) >> 4
    for q in range(PLANES * PAIRS // 4):
        first = last = None
        for s in range(4):
            d, g = divmod(4 * q + s, PAIRS)
            x = chunks[d][g]
            if g < 3:
                x = x + src[d, g]
            a = roll_lanes(x, 16 * s)
            b = roll_lanes(x, 16 * s + 80)
            first = a if s == 0 else jnp.where(slot == s, a, first)
            last = b if s == 0 else jnp.where(slot == s, b, last)
        first_ref[q] = first
        last_ref[q] = last


def block_apply(blocks, v):
    return [blocks[3 * a] * v[0] + blocks[3 * a + 1] * v[1] + blocks[3 * a + 2] * v[2] for a in range(3)]


def plane_apply(blocks, lower, upper, v):
    w = block_apply(blocks, v)
    u = [v[c] - lower[c] * roll_lanes(w[c], 1) - upper[c] * roll_lanes(w[c], 127) for c in range(3)]
    return block_apply(blocks, u)


def march_kernel(me_ref, *rest):
    chunks, rest = rest[:PLANES], rest[PLANES:]
    zrefs, rest = rest[:PLANES], rest[PLANES:]
    (src, before, after, pick_ref), rest = rest[:4], rest[4:]
    outs, (grid, field) = rest[:PLANES], rest[PLANES:]
    me = me_ref[0]
    lane = lane_iota(ZC)
    own = lane < 64
    right = lane < 80
    left = lane >= 112

    for d in range(PLANES):
        plane = (me - d) & 7
        for g in range(PAIRS):
            q, s = divmod(PAIRS * d + g, 4)
            x = chunks[d][g]
            if g < 3:
                x = x + src[d, g]
            for h in range(2):
                n = 2 * g + h
                if n == 27:
                    continue
                at = 16 * s + 64 * h
                edge = jnp.where(right, roll_lanes(after[q], 64 - at), roll_lanes(before[q], 112 - at))
                edge = jnp.where(jnp.logical_or(right, left), edge, 0.0)
                grid[plane, n] = jnp.where(own, roll_lanes(x, 64 * h), edge)

    for t in range(2):
        rows = slice(8 * t, 8 * t + 8)
        state = None
        for i in range(PLANES):
            blocks = [grid[i, 6 + n, rows] for n in range(9)]
            lower = [grid[i, 21 + c, rows] for c in range(3)]
            upper = [grid[i, 24 + c, rows] for c in range(3)]
            new = []
            for k in range(2):
                v = [grid[i, 3 * k + c, rows] for c in range(3)]
                if i > 0:
                    v = [v[c] - grid[i, 15 + c, rows] * state[k][c] for c in range(3)]
                new.append(plane_apply(blocks, lower, upper, v))
            state = new
            for k in range(2):
                for c in range(3):
                    field[i, 3 * k + c, rows] = state[k][c]
        for i in range(PLANES - 2, -1, -1):
            blocks = [grid[i, 6 + n, rows] for n in range(9)]
            lower = [grid[i, 21 + c, rows] for c in range(3)]
            upper = [grid[i, 24 + c, rows] for c in range(3)]
            new = []
            for k in range(2):
                v = [grid[i, 18 + c, rows] * state[k][c] for c in range(3)]
                p = plane_apply(blocks, lower, upper, v)
                new.append([field[i, 3 * k + c, rows] - p[c] for c in range(3)])
            state = new
            for k in range(2):
                for c in range(3):
                    field[i, 3 * k + c, rows] = state[k][c]

    for d in range(PLANES):
        plane = (me + d) & 7
        for c in range(3):
            pair = jnp.where(own, field[plane, c], roll_lanes(field[plane, 3 + c], 64))
            outs[d][2 * c] = pair[0:8]
            outs[d][2 * c + 1] = pair[8:16]

    tiles = perf_tiles(zrefs)
    row = row_iota(128)
    depth_row = row_iota(ZC)
    half = lane_iota(1) < 64
    parts = []
    for j in range(4):
        cell = tiles[j][3:4].astype(jnp.int32)
        at_z = (cell & 127) == depth_row + me * ZC
        at_y = jnp.where(((cell >> 7) & 63) == row, 1.0, 0.0).astype(BF16)
        total = None
        for side in range(2):
            plane = (me - 2 * j - side) & 7
            x = jnp.concatenate([field[plane, 3 + c] for c in range(3)], axis=0)
            got = join_rows(jnp.dot(split_rows(x), at_y, preferred_element_type=F32), 48)
            keep = jnp.logical_and(at_z, half if side == 0 else jnp.logical_not(half))
            got = [jnp.where(keep, got[16 * c : 16 * c + 16], 0.0) for c in range(3)]
            total = got if total is None else [a + b for a, b in zip(total, got)]
        value = [jnp.sum(t, axis=0, keepdims=True) * tiles[j][5:6] for t in total]
        value = jnp.concatenate(value + [jnp.zeros((5, 128), F32)], axis=0)
        parts.append(
            jnp.concatenate(list(split3(value)) + [jnp.zeros((8, 128), F32)], axis=0).astype(BF16)
        )
    parts = jnp.concatenate(parts, axis=1)
    for d in range(PLANES):
        sums = lax.dot_general(
            parts, pick_ref[(PLANES - d) % PLANES], (((1,), (1,)), ((), ())), preferred_element_type=F32
        )
        outs[d][6] = join_rows(sums, 8)


def unpack_kernel(me_ref, *rest):
    chunks, (out, turned) = rest[:PLANES], rest[PLANES:]
    me = me_ref[0]
    for d in range(PLANES):
        start = ((me - d) & 7) * ZC
        for c in range(3):
            for t in range(2):
                turned[c, pl.ds(pl.multiple_of(start + 8 * t, 8), 8), :] = chunks[d][2 * c + t]
    for c in range(3):
        y = turned[c].T
        out[0, c] = y[0:LINES]
        out[1, c] = y[LINES : 2 * LINES]


def call(kernel, inputs, out_shape, scratch=()):
    return pl.pallas_call(
        kernel,
        out_shape=out_shape,
        in_specs=[SMEM if x.ndim == 1 else VMEM for x in inputs],
        out_specs=jax.tree.map(lambda _: VMEM, out_shape),
        scratch_shapes=list(scratch),
        compiler_params=pltpu.CompilerParams(vmem_limit_bytes=VMEM_LIMIT),
    )(*inputs)


def shift_gx(x, d):
    n = lax.axis_size("gx")
    return lax.ppermute(x, "gx", [(i, (i + d) % n) for i in range(n)])


def radices(size):
    out = []
    while size > 1:
        r = 4 if size % 4 == 0 and size != 8 else 2
        out.append(r)
        size //= r
    return out


def sum_gy(x):
    size = lax.axis_size("gy")
    stride = 1
    for radix in reversed(radices(size)):
        total = x
        for k in range(1, radix):
            route = []
            for b in range(size):
                digit = (b // stride) % radix
                route.append((b, b + ((digit + k) % radix - digit) * stride))
            total = total + lax.ppermute(x, "gy", route)
        x = total
        stride *= radix
    return x


EXCHANGE_ORDER = (4, 3, 5, 2, 6, 1, 7)


def per_device(
    adjoint_rhs, block_inverse, x_couplings, y_couplings, perf_cell, perf_well, perf_weight, well_adjoint
):
    me = lax.axis_index("gx").astype(jnp.int32)
    line_block = lax.axis_index("gy")
    me_arr = me.reshape(1)
    held = well_adjoint.shape[1]

    chunk = jax.ShapeDtypeStruct((PAIRS, ZC, 128), F32)
    packed = call(
        pack_kernel,
        [
            me_arr,
            adjoint_rhs.reshape(6, LINES, 128),
            block_inverse.reshape(9, LINES, 128),
            x_couplings.reshape(6, LINES, 128),
            y_couplings.reshape(6, LINES, 128),
        ],
        [chunk] * PLANES,
        [pltpu.VMEM((PAIRS, 128, 128), F32)],
    )
    chunks = [packed[0]] + [None] * 7
    for d in EXCHANGE_ORDER:
        chunks[d] = shift_gx(packed[d], d)

    wells = lax.dynamic_update_slice(jnp.zeros((8, 128), F32), well_adjoint, (0, held * line_block))
    wells = sum_gy(wells)
    perfs = jnp.stack([perf_cell.astype(F32), perf_well.astype(F32), perf_weight])
    wells = wells + jnp.pad(perfs, ((3, 2), (0, 64)))
    tiles = [wells] + [shift_gx(wells, d) for d in range(1, PLANES)]

    src, pick = call(
        source_kernel,
        [me_arr] + tiles,
        [
            jax.ShapeDtypeStruct((PLANES, 3, ZC, 128), F32),
            jax.ShapeDtypeStruct((PLANES, 128, 512), BF16),
        ],
    )

    strip = jax.ShapeDtypeStruct((PLANES * PAIRS // 4, ZC, 128), F32)
    first, last = call(strip_kernel, chunks + [src], [strip, strip])
    lines = lax.axis_size("gy")
    up = [(i, i + 1) for i in range(lines - 1)]
    before = lax.ppermute(last, "gy", up)
    after = lax.ppermute(first, "gy", [(j, i) for i, j in up])

    back = call(
        march_kernel,
        [me_arr] + chunks + tiles + [src, before, after, pick],
        [jax.ShapeDtypeStruct((7, 8, 128), F32)] * PLANES,
        [pltpu.VMEM((PLANES, 27, ZC, 128), F32), pltpu.VMEM((PLANES, 6, ZC, 128), F32)],
    )
    got = [back[0]] + [None] * 7
    for d in EXCHANGE_ORDER:
        got[d] = shift_gx(back[d], d)

    precond = call(
        unpack_kernel,
        [me_arr] + got,
        jax.ShapeDtypeStruct((2, 3, LINES, 128), F32),
        [pltpu.VMEM((3, 128, 128), F32)],
    ).reshape(adjoint_rhs.shape)
    sums = got[0][6]
    for d in range(1, PLANES):
        sums = sums + got[d][6]
    sums = sum_gy(sums)
    well_update = lax.dynamic_slice(sums, (0, held * line_block), (3, held))
    return precond, well_update


def solution(mesh):
    placed = (
        P(None, None, "gx", "gy", None),
        P(None, None, "gx", "gy", None),
        P(None, None, "gx", "gy", None),
        P(None, None, "gx", "gy", None),
        P(("gx", "gy")),
        P(("gx", "gy")),
        P(("gx", "gy")),
        P(None, ("gx", "gy")),
    )
    return jax.shard_map(
        per_device,
        mesh=mesh,
        in_specs=placed,
        out_specs=(P(None, None, "gx", "gy", None), P(None, ("gx", "gy"))),
        check_vma=False,
    )
```

```python
import functools

import jax
import jax.numpy as jnp
from jax import lax
from jax.experimental import pallas as pl
from jax.experimental.pallas import tpu as pltpu
from jax.sharding import PartitionSpec as P

F32 = jnp.float32
BF16 = jnp.bfloat16
PLANES = 8
LINES = 64
ZC = 16
PAIRS = 14
STRIP = 16
WELL_ROW = 3
VMEM_LIMIT = 24 * 1024 * 1024

VMEM = pl.BlockSpec(memory_space=pltpu.VMEM)


def split3(x):
    hi = x.astype(BF16).astype(F32)
    rest = x - hi
    mid = rest.astype(BF16).astype(F32)
    lo = rest - mid
    return hi, mid, lo


def split_rows(x):
    return jnp.concatenate(split3(x), axis=0).astype(BF16)


def join_rows(y, rows):
    return y[0:rows] + y[rows : 2 * rows] + y[2 * rows : 3 * rows]


def lane_iota(rows):
    return lax.broadcasted_iota(jnp.int32, (rows, 128), 1)


def row_iota(rows):
    return lax.broadcasted_iota(jnp.int32, (rows, 128), 0)


def roll_lanes(x, shift):
    shift %= 128
    return x if shift == 0 else pltpu.roll(x, shift, 1)


def wells_kernel(wells, out, wide):
    held = wells.shape[1]
    wide[...] = jnp.zeros_like(wide)
    wide[0:3, 0:held] = wells[...]
    row = jnp.zeros((1, 128), F32)
    for c in range(3):
        row = row + roll_lanes(wide[c : c + 1], WELL_ROW + held * c)
    out[...] = jnp.broadcast_to(row, out.shape)


def pack_kernel(rhs, einv, xc, yc, cell, well, weight, wells, *rest):
    out, rhs_v, einv_v, xc_v, yc_v, cell_v, well_v, weight_v, wells_v, turned, sems = rest
    moves = [
        pltpu.make_async_copy(src, dst, sems.at[i])
        for i, (src, dst) in enumerate(
            [
                (rhs, rhs_v),
                (einv, einv_v),
                (xc, xc_v),
                (yc, yc_v),
                (cell, cell_v),
                (well, well_v),
                (weight, weight_v),
                (wells, wells_v),
            ]
        )
    ]
    for move in moves:
        move.start()
    arrays = (
        [(rhs_v, 0, i) for i in range(6)]
        + [(einv_v, 1, i) for i in range(9)]
        + [(xc_v, 2, i) for i in range(6)]
        + [(yc_v, 3, i) for i in range(6)]
    )
    waited = -1
    for g in range(PAIRS):
        ends = []
        for n in (2 * g, 2 * g + 1):
            if n == 27:
                ends.append(jnp.zeros((LINES, 128), F32))
                continue
            ref, stage, i = arrays[n]
            if stage > waited:
                moves[stage].wait()
                waited = stage
            ends.append(ref[i])
        turned[g] = jnp.concatenate(ends, axis=0).T
    for stage in (4, 5, 6, 7):
        moves[stage].wait()
    perfs = jnp.concatenate(
        [cell_v[...].astype(F32), well_v[...].astype(F32), weight_v[...], jnp.zeros((ZC - 3, LINES), F32)], axis=0
    )
    lines = wells_v.shape[0]
    gathered = jnp.concatenate([wells_v[...], jnp.zeros((128 - lines, 128), F32)], axis=0).T[0:ZC]
    perfs = jnp.concatenate([jnp.zeros((ZC, 64), F32), perfs], axis=1) + roll_lanes(gathered, 64)
    low = lane_iota(ZC) < 64
    for t in range(PLANES):
        rows = slice(ZC * t, ZC * t + ZC)
        for g in range(PAIRS - 1):
            out[t, g] = turned[g, rows, :]
        out[t, PAIRS - 1] = jnp.where(low, turned[PAIRS - 1, rows, :], perfs)


def perf_tiles(chunks):
    low = lane_iota(8) < 64
    last = PAIRS - 1
    return [
        jnp.where(low, roll_lanes(chunks[2 * j, last, 0:8], 64), chunks[2 * j + 1, last, 0:8])
        for j in range(PLANES // 2)
    ]


def ints(row):
    return row.astype(jnp.int32)


def place_of(tile, first_z):
    cell = ints(tile[0:1])
    at_z = (cell & 127) == row_iota(ZC) + first_z
    at_y = jnp.where(((cell >> 7) & 63) == row_iota(128), 1.0, 0.0).astype(BF16)
    return at_z, at_y


def sides(at_z):
    low = lane_iota(ZC) < 64
    return [jnp.logical_and(at_z, low), jnp.logical_and(at_z, jnp.logical_not(low))]


def strip_kernel(line_bits, held, chunks, first_ref, last_ref, src_ref):
    bits = held.bit_length() - 1
    lines = 1 << line_bits
    me = lax.axis_index("gx")
    tiles = perf_tiles(chunks)
    place = lane_iota(ZC) >> 5
    wells = []
    for u in range(2):
        tile = None
        for v in range(4):
            part = roll_lanes(chunks[4 * u + v, PAIRS - 1], 32 * v - 64)
            tile = part if v == 0 else jnp.where(place == v, part, tile)
        wells.append(tile)
    wells = split_rows(jnp.concatenate(wells, axis=1))
    low = lane_iota(ZC) < 64
    for j in range(PLANES // 2):
        well = ints(tiles[j][1:2])
        owner = well >> bits
        at = (owner >> line_bits) * 32 + (owner & (lines - 1))
        hot = jnp.where(at == row_iota(256), 1.0, 0.0).astype(BF16)
        picked = join_rows(jnp.dot(wells, hot, preferred_element_type=F32), ZC)
        terms = []
        for c in range(3):
            term = jnp.zeros((1, 128), F32)
            for i in range(held):
                term = jnp.where((well & (held - 1)) == i, picked[WELL_ROW + held * c + i : WELL_ROW + held * c + i + 1], term)
            terms.append(term * tiles[j][2:3])
        at_z, at_y = place_of(tiles[j], me * ZC)
        rows = [jnp.where(keep, term, 0.0) for keep in sides(at_z) for term in terms]
        left = split_rows(jnp.concatenate(rows, axis=0))
        spread = lax.dot_general(left, at_y, (((1,), (1,)), ((), ())), preferred_element_type=F32)
        spread = join_rows(spread, 96)
        for side in range(2):
            c0, c1, c2 = (spread[48 * side + 16 * c : 48 * side + 16 * c + 16] for c in range(3))
            d = 2 * j + side
            src_ref[d, 0] = jnp.where(low, c0, roll_lanes(c1, 64))
            src_ref[d, 1] = jnp.where(low, c2, roll_lanes(c0, 64))
            src_ref[d, 2] = jnp.where(low, c1, roll_lanes(c2, 64))
    slot = (lane_iota(ZC) & 63) >> 4
    for q in range(PLANES * PAIRS // 4):
        first = last = None
        for s in range(4):
            d, g = divmod(4 * q + s, PAIRS)
            x = chunks[d, g]
            if g < 3:
                x = x + src_ref[d, g]
            a = roll_lanes(x, 16 * s)
            b = roll_lanes(x, 16 * s + 80)
            first = a if s == 0 else jnp.where(slot == s, a, first)
            last = b if s == 0 else jnp.where(slot == s, b, last)
        first_ref[q] = first
        last_ref[q] = last


def block_apply(blocks, v):
    return [blocks[3 * a] * v[0] + blocks[3 * a + 1] * v[1] + blocks[3 * a + 2] * v[2] for a in range(3)]


def plane_apply(blocks, lower, upper, v):
    w = block_apply(blocks, v)
    u = [v[c] - lower[c] * roll_lanes(w[c], 1) - upper[c] * roll_lanes(w[c], 127) for c in range(3)]
    return block_apply(blocks, u)


def march_kernel(share, chunks, src, before, after, out_ref, grid, field):
    me = lax.axis_index("gx")
    lane = lane_iota(ZC)
    own = lane < 64
    right = lane < 80
    left = lane >= 112

    for d in range(PLANES):
        for g in range(PAIRS):
            q, s = divmod(PAIRS * d + g, 4)
            x = chunks[d, g]
            if g < 3:
                x = x + src[d, g]
            for h in range(2):
                n = 2 * g + h
                if n == 27:
                    continue
                at = 16 * s + 64 * h
                edge = jnp.where(right, roll_lanes(after[q], 64 - at), roll_lanes(before[q], 112 - at))
                edge = jnp.where(jnp.logical_or(right, left), edge, 0.0)
                grid[d, n] = jnp.where(own, roll_lanes(x, 64 * h), edge)

    for t in range(2):
        rows = slice(8 * t, 8 * t + 8)
        state = None
        for i in range(PLANES):
            blocks = [grid[i, 6 + n, rows] for n in range(9)]
            lower = [grid[i, 21 + c, rows] for c in range(3)]
            upper = [grid[i, 24 + c, rows] for c in range(3)]
            new = []
            for k in range(2):
                v = [grid[i, 3 * k + c, rows] for c in range(3)]
                if i > 0:
                    v = [v[c] - grid[i, 15 + c, rows] * state[k][c] for c in range(3)]
                new.append(plane_apply(blocks, lower, upper, v))
            state = new
            for k in range(2):
                for c in range(3):
                    field[i, 3 * k + c, rows] = state[k][c]
        for i in range(PLANES - 2, -1, -1):
            blocks = [grid[i, 6 + n, rows] for n in range(9)]
            lower = [grid[i, 21 + c, rows] for c in range(3)]
            upper = [grid[i, 24 + c, rows] for c in range(3)]
            new = []
            for k in range(2):
                v = [grid[i, 18 + c, rows] * state[k][c] for c in range(3)]
                p = plane_apply(blocks, lower, upper, v)
                new.append([field[i, 3 * k + c, rows] - p[c] for c in range(3)])
            state = new
            for k in range(2):
                for c in range(3):
                    field[i, 3 * k + c, rows] = state[k][c]

    for i in range(PLANES):
        for c in range(3):
            pair = jnp.where(own, field[i, c], roll_lanes(field[i, 3 + c], 64))
            out_ref[i, 2 * c] = pair[0:8]
            out_ref[i, 2 * c + 1] = pair[8:16]

    tiles = perf_tiles(chunks)
    parts = []
    for j in range(PLANES // 2):
        at_z, at_y = place_of(tiles[j], me * ZC)
        found = None
        for side, keep in enumerate(sides(at_z)):
            x = jnp.concatenate([field[2 * j + side, 3 + c] for c in range(3)], axis=0)
            got = join_rows(jnp.dot(split_rows(x), at_y, preferred_element_type=F32), 48)
            got = [jnp.where(keep, got[16 * c : 16 * c + 16], 0.0) for c in range(3)]
            found = got if found is None else [a + b for a, b in zip(found, got)]
        value = [jnp.sum(f, axis=0, keepdims=True) * tiles[j][2:3] for f in found]
        value = jnp.concatenate(value + [jnp.zeros((5, 128), F32)], axis=0)
        parts.append(jnp.concatenate(list(split3(value)) + [jnp.zeros((8, 128), F32)], axis=0).astype(BF16))
    wells = [ints(tile[1:2]) for tile in tiles]
    row = row_iota(128)
    for i in range(PLANES):
        total = jnp.zeros((32, 128), F32)
        for j in range(PLANES // 2):
            hot = jnp.where(wells[j] == row + share * i, 1.0, 0.0).astype(BF16)
            total += lax.dot_general(parts[j], hot, (((1,), (1,)), ((), ())), preferred_element_type=F32)
        out_ref[i, 6] = join_rows(total, 8)


def unpack_kernel(chunks, out, sums, turned):
    total = chunks[0, 6]
    for t in range(1, PLANES):
        total = total + chunks[t, 6]
    sums[...] = jnp.broadcast_to(total[None], sums.shape)
    for t in range(PLANES):
        for c in range(3):
            for h in range(2):
                turned[c, ZC * t + 8 * h : ZC * t + 8 * h + 8] = chunks[t, 2 * c + h]
    for c in range(3):
        y = turned[c].T
        out[0, c] = y[0:LINES]
        out[1, c] = y[LINES : 2 * LINES]


def final_kernel(sums, out):
    held = out.shape[1]
    total = sums[0]
    for b in range(1, sums.shape[0]):
        total = total + sums[b]
    shift = (128 - held * lax.axis_index("gy")) & 127
    out[...] = pltpu.roll(total, shift, 1)[0:3, 0:held]


def call(kernel, inputs, out_shape, scratch=(), space=VMEM):
    if space is not VMEM:
        inputs = [pltpu.with_memory_space_constraint(x, space) for x in inputs]
        space = pl.BlockSpec(memory_space=space)
    return pl.pallas_call(
        kernel,
        out_shape=out_shape,
        in_specs=[space] * len(inputs),
        out_specs=jax.tree.map(lambda _: VMEM, out_shape),
        scratch_shapes=list(scratch),
        compiler_params=pltpu.CompilerParams(vmem_limit_bytes=VMEM_LIMIT),
    )(*inputs)


def shape(*dims):
    return jax.ShapeDtypeStruct(dims, F32)


def per_device(
    adjoint_rhs, block_inverse, x_couplings, y_couplings, perf_cell, perf_well, perf_weight, well_adjoint
):
    held = well_adjoint.shape[1]
    lines = lax.axis_size("gy")
    perfs = perf_cell.shape[0]

    row = call(wells_kernel, [well_adjoint], shape(lines, 128), [pltpu.VMEM((8, 128), F32)])
    wells = lax.all_to_all(row, "gy", 0, 0, tiled=True)

    packed = call(
        pack_kernel,
        [
            adjoint_rhs.reshape(6, LINES, 128),
            block_inverse.reshape(9, LINES, 128),
            x_couplings.reshape(6, LINES, 128),
            y_couplings.reshape(6, LINES, 128),
            perf_cell.reshape(1, perfs),
            perf_well.reshape(1, perfs),
            perf_weight.reshape(1, perfs),
            wells,
        ],
        shape(PLANES, PAIRS, ZC, 128),
        [
            pltpu.VMEM((6, LINES, 128), F32),
            pltpu.VMEM((9, LINES, 128), F32),
            pltpu.VMEM((6, LINES, 128), F32),
            pltpu.VMEM((6, LINES, 128), F32),
            pltpu.VMEM((1, perfs), jnp.int32),
            pltpu.VMEM((1, perfs), jnp.int32),
            pltpu.VMEM((1, perfs), F32),
            pltpu.VMEM((lines, 128), F32),
            pltpu.VMEM((PAIRS, 128, 128), F32),
            pltpu.SemaphoreType.DMA((8,)),
        ],
        space=pltpu.HBM,
    )
    chunks = lax.all_to_all(packed, "gx", 0, 0)

    strip = shape(PLANES * PAIRS // 4, ZC, 128)
    first, last, src = call(
        functools.partial(strip_kernel, lines.bit_length() - 1, held),
        [chunks],
        [strip, strip, shape(PLANES, 3, ZC, 128)],
    )
    up = [(i, i + 1) for i in range(lines - 1)]
    before = lax.ppermute(last, "gy", up)
    after = lax.ppermute(first, "gy", [(j, i) for i, j in up])

    back = call(
        functools.partial(march_kernel, held * lines),
        [chunks, src, before, after],
        shape(PLANES, 7, 8, 128),
        [pltpu.VMEM((PLANES, 27, ZC, 128), F32), pltpu.VMEM((PLANES, 6, ZC, 128), F32)],
    )
    got = lax.all_to_all(back, "gx", 0, 0)
    precond, sums = call(
        unpack_kernel,
        [got],
        [shape(2, 3, LINES, 128), shape(lines, 8, 128)],
        [pltpu.VMEM((3, 128, 128), F32)],
    )
    sums = lax.all_to_all(sums, "gy", 0, 0)
    well_update = call(final_kernel, [sums], shape(3, held))
    return precond.reshape(adjoint_rhs.shape), well_update


def solution(mesh):
    placed = (
        P(None, None, "gx", "gy", None),
        P(None, None, "gx", "gy", None),
        P(None, None, "gx", "gy", None),
        P(None, None, "gx", "gy", None),
        P(("gx", "gy")),
        P(("gx", "gy")),
        P(("gx", "gy")),
        P(None, ("gx", "gy")),
    )
    return jax.shard_map(
        per_device,
        mesh=mesh,
        in_specs=placed,
        out_specs=(P(None, None, "gx", "gy", None), P(None, ("gx", "gy"))),
        check_vma=False,
    )
```

```python
import functools

import jax
import jax.numpy as jnp
from jax import lax
from jax.experimental import pallas as pl
from jax.experimental.pallas import tpu as pltpu
from jax.sharding import PartitionSpec as P

F32 = jnp.float32
BF16 = jnp.bfloat16
PLANES = 8
LINES = 64
ZC = 16
PAIRS = 14
STRIP = 16
WELL_ROW = 3
STRIPS = PLANES * PAIRS // 4
VMEM_LIMIT = 24 * 1024 * 1024

VMEM = pl.BlockSpec(memory_space=pltpu.VMEM)


def split3(x):
    hi = x.astype(BF16).astype(F32)
    rest = x - hi
    mid = rest.astype(BF16).astype(F32)
    lo = rest - mid
    return hi, mid, lo


def split_rows(x):
    return jnp.concatenate(split3(x), axis=0).astype(BF16)


def join_rows(y, rows):
    return y[0:rows] + y[rows : 2 * rows] + y[2 * rows : 3 * rows]


def lane_iota(rows):
    return lax.broadcasted_iota(jnp.int32, (rows, 128), 1)


def row_iota(rows):
    return lax.broadcasted_iota(jnp.int32, (rows, 128), 0)


def roll_lanes(x, shift):
    shift %= 128
    return x if shift == 0 else pltpu.roll(x, shift, 1)


def pack_kernel(rhs, einv, xc, yc, cell, well, weight, wells, *rest):
    out, rhs_v, einv_v, xc_v, yc_v, cell_v, well_v, weight_v, wells_v, wide, turned, sems = rest
    moves = [
        pltpu.make_async_copy(src, dst, sems.at[i])
        for i, (src, dst) in enumerate(
            [
                (rhs, rhs_v),
                (einv, einv_v),
                (xc, xc_v),
                (yc, yc_v),
                (cell, cell_v),
                (well, well_v),
                (weight, weight_v),
                (wells, wells_v),
            ]
        )
    ]
    for move in moves:
        move.start()
    arrays = (
        [(rhs_v, 0, i) for i in range(6)]
        + [(einv_v, 1, i) for i in range(9)]
        + [(xc_v, 2, i) for i in range(6)]
        + [(yc_v, 3, i) for i in range(6)]
    )
    waited = -1
    for g in range(PAIRS):
        ends = []
        for n in (2 * g, 2 * g + 1):
            if n == 27:
                ends.append(jnp.zeros((LINES, 128), F32))
                continue
            ref, stage, i = arrays[n]
            if stage > waited:
                moves[stage].wait()
                waited = stage
            ends.append(ref[i])
        turned[g] = jnp.concatenate(ends, axis=0).T
    for stage in (4, 5, 6, 7):
        moves[stage].wait()
    held = wells_v.shape[1]
    wide[...] = jnp.zeros_like(wide)
    wide[0, 0:LINES] = cell_v[0].astype(F32)
    wide[1, 0:LINES] = well_v[0].astype(F32)
    wide[2, 0:LINES] = weight_v[0]
    wide[8:11, 0:held] = wells_v[...]
    own = wide[8:9] + roll_lanes(wide[9:10], held) + roll_lanes(wide[10:11], 2 * held)
    wide[8:11] = jnp.zeros((3, 128), F32)
    wide[WELL_ROW : WELL_ROW + 1] = own
    perfs = roll_lanes(wide[...], 64)
    low = lane_iota(ZC) < 64
    for t in range(PLANES):
        rows = slice(ZC * t, ZC * t + ZC)
        for g in range(PAIRS - 1):
            out[t, g] = turned[g, rows, :]
        out[t, PAIRS - 1] = jnp.where(low, turned[PAIRS - 1, rows, :], perfs)


def perf_tiles(chunks):
    low = lane_iota(8) < 64
    last = PAIRS - 1
    return [
        jnp.where(low, roll_lanes(chunks[2 * j, last, 0:8], 64), chunks[2 * j + 1, last, 0:8])
        for j in range(PLANES // 2)
    ]


def ints(row):
    return row.astype(jnp.int32)


def place_of(tile, first_z):
    cell = ints(tile[0:1])
    at_z = (cell & 127) == row_iota(ZC) + first_z
    at_y = jnp.where(((cell >> 7) & 63) == row_iota(128), 1.0, 0.0).astype(BF16)
    return at_z, at_y


def on_even():
    return jnp.zeros((ZC, 128), jnp.int32) + (lax.axis_index("gy") & 1) == 0


def sides(at_z):
    low = lane_iota(ZC) < 64
    return [jnp.logical_and(at_z, low), jnp.logical_and(at_z, jnp.logical_not(low))]


def strip_kernel(chunks, near_ref, far_ref, wells_ref):
    last = PAIRS - 1
    own = jnp.concatenate([chunks[d, last, WELL_ROW : WELL_ROW + 1] for d in range(PLANES)], axis=0)
    wells_ref[...] = jnp.broadcast_to(roll_lanes(own, 64)[None], wells_ref.shape)
    tiles = perf_tiles(chunks)
    for u in range(2):
        pair = jnp.concatenate([tiles[2 * u], tiles[2 * u + 1]], axis=0)
        near_ref[STRIPS + u] = pair
        far_ref[STRIPS + u] = pair
    slot = (lane_iota(ZC) & 63) >> 4
    even = on_even()
    for q in range(PLANES * PAIRS // 4):
        first = last = None
        for s in range(4):
            d, g = divmod(4 * q + s, PAIRS)
            x = chunks[d, g]
            a = roll_lanes(x, 16 * s)
            b = roll_lanes(x, 16 * s + 80)
            first = a if s == 0 else jnp.where(slot == s, a, first)
            last = b if s == 0 else jnp.where(slot == s, b, last)
        near_ref[q] = jnp.where(even, last, first)
        far_ref[q] = jnp.where(even, first, last)


def block_apply(blocks, v):
    return [blocks[3 * a] * v[0] + blocks[3 * a + 1] * v[1] + blocks[3 * a + 2] * v[2] for a in range(3)]


def plane_apply(blocks, lower, upper, v):
    w = block_apply(blocks, v)
    u = [v[c] - lower[c] * roll_lanes(w[c], 1) - upper[c] * roll_lanes(w[c], 127) for c in range(3)]
    return block_apply(blocks, u)


def sources(line_bits, bits, chunks, wells_ref, near, far, src):
    held = 1 << bits
    first_z = lax.axis_index("gx") * ZC
    wells = split_rows(wells_ref[...].reshape(-1, 128).T[0:ZC])
    own = perf_tiles(chunks)
    row = row_iota(128)
    odd = lax.axis_index("gy") & 1
    start = [64 + 48 * odd, 112 - 48 * odd]
    spans = [row < 64] + [jnp.logical_and(row >= first, row < first + 16) for first in start]
    for j in range(PLANES // 2):
        half = slice(8 * (j % 2), 8 * (j % 2) + 8)
        total = None
        for tile, span, base in zip([own[j], near[STRIPS + j // 2, half], far[STRIPS + j // 2, half]], spans, (0, 64, 64)):
            well = ints(tile[1:2])
            owner = well >> bits
            at = (owner & ((1 << line_bits) - 1)) * PLANES + (owner >> line_bits)
            hot = jnp.where(at == row_iota(wells.shape[1]), 1.0, 0.0).astype(BF16)
            picked = join_rows(jnp.dot(wells, hot, preferred_element_type=F32), ZC)
            terms = []
            for c in range(3):
                term = jnp.zeros((1, 128), F32)
                for i in range(held):
                    term = jnp.where((well & (held - 1)) == i, picked[held * c + i : held * c + i + 1], term)
                terms.append(term * tile[2:3])
            cell = ints(tile[0:1])
            at_z = (cell & 127) == row_iota(ZC) + first_z
            at_y = ((cell >> 7) & 63) + base == row
            at_y = jnp.where(jnp.logical_and(at_y, span), 1.0, 0.0).astype(BF16)
            rows = [jnp.where(keep, term, 0.0) for keep in sides(at_z) for term in terms]
            rows = split_rows(jnp.concatenate(rows, axis=0))
            spread = lax.dot_general(rows, at_y, (((1,), (1,)), ((), ())), preferred_element_type=F32)
            total = spread if total is None else total + spread
        total = join_rows(total, 6 * ZC)
        for side in range(2):
            for c in range(3):
                src[2 * j + side, c] = total[(3 * side + c) * ZC : (3 * side + c + 1) * ZC]


def march_kernel(line_bits, bits, chunks, wells_ref, near, far, out_ref, grid, field, src):
    share = 1 << (line_bits + bits)
    me = lax.axis_index("gx")
    sources(line_bits, bits, chunks, wells_ref, near, far, src)
    lane = lane_iota(ZC)
    own = lane < 64
    right = lane < 80
    even = on_even()
    left = lane >= 112

    for d in range(PLANES):
        for g in range(PAIRS):
            q, s = divmod(PAIRS * d + g, 4)
            x = chunks[d, g]
            after = jnp.where(even, near[q], far[q])
            before = jnp.where(even, far[q], near[q])
            for h in range(2):
                n = 2 * g + h
                if n == 27:
                    continue
                at = 16 * s + 64 * h
                edge = jnp.where(right, roll_lanes(after, 64 - at), roll_lanes(before, 112 - at))
                edge = jnp.where(jnp.logical_or(right, left), edge, 0.0)
                value = jnp.where(own, roll_lanes(x, 64 * h), edge)
                if n < 6:
                    value = value + src[d, n % 3]
                grid[d, n] = value

    state = None
    for i in range(PLANES):
        blocks = [grid[i, 6 + n] for n in range(9)]
        lower = [grid[i, 21 + c] for c in range(3)]
        upper = [grid[i, 24 + c] for c in range(3)]
        new = []
        for k in range(2):
            v = [grid[i, 3 * k + c] for c in range(3)]
            if i > 0:
                v = [v[c] - grid[i, 15 + c] * state[k][c] for c in range(3)]
            new.append(plane_apply(blocks, lower, upper, v))
        state = new
        for k in range(2):
            for c in range(3):
                field[i, 3 * k + c] = state[k][c]
    for i in range(PLANES - 2, -1, -1):
        blocks = [grid[i, 6 + n] for n in range(9)]
        lower = [grid[i, 21 + c] for c in range(3)]
        upper = [grid[i, 24 + c] for c in range(3)]
        new = []
        for k in range(2):
            v = [grid[i, 18 + c] * state[k][c] for c in range(3)]
            p = plane_apply(blocks, lower, upper, v)
            new.append([field[i, 3 * k + c] - p[c] for c in range(3)])
        state = new
        for k in range(2):
            for c in range(3):
                field[i, 3 * k + c] = state[k][c]

    for i in range(PLANES):
        for c in range(3):
            pair = jnp.where(own, field[i, c], roll_lanes(field[i, 3 + c], 64))
            out_ref[i, 2 * c] = pair[0:8]
            out_ref[i, 2 * c + 1] = pair[8:16]

    tiles = perf_tiles(chunks)
    parts = []
    for j in range(PLANES // 2):
        at_z, at_y = place_of(tiles[j], me * ZC)
        found = None
        for side, keep in enumerate(sides(at_z)):
            x = jnp.concatenate([field[2 * j + side, 3 + c] for c in range(3)], axis=0)
            got = join_rows(jnp.dot(split_rows(x), at_y, preferred_element_type=F32), 48)
            got = [jnp.where(keep, got[16 * c : 16 * c + 16], 0.0) for c in range(3)]
            found = got if found is None else [a + b for a, b in zip(found, got)]
        value = [jnp.sum(f, axis=0, keepdims=True) * tiles[j][2:3] for f in found]
        value = jnp.concatenate(value + [jnp.zeros((5, 128), F32)], axis=0)
        parts.append(jnp.concatenate(list(split3(value)) + [jnp.zeros((8, 128), F32)], axis=0).astype(BF16))
    wells = [ints(tile[1:2]) for tile in tiles]
    row = row_iota(128)
    for i in range(PLANES):
        total = jnp.zeros((32, 128), F32)
        for j in range(PLANES // 2):
            hot = jnp.where(wells[j] == row + share * i, 1.0, 0.0).astype(BF16)
            total += lax.dot_general(parts[j], hot, (((1,), (1,)), ((), ())), preferred_element_type=F32)
        out_ref[i, 6] = join_rows(total, 8)


def unpack_kernel(chunks, sums, out, wells, turned):
    held = wells.shape[1]
    total = sums[0]
    for b in range(1, sums.shape[0]):
        total = total + sums[b]
    shift = (128 - held * lax.axis_index("gy")) & 127
    wells[...] = pltpu.roll(total, shift, 1)[0:3, 0:held]
    for t in range(PLANES):
        for c in range(3):
            for h in range(2):
                turned[c, ZC * t + 8 * h : ZC * t + 8 * h + 8] = chunks[t, 2 * c + h]
    for c in range(3):
        y = turned[c].T
        out[0, c] = y[0:LINES]
        out[1, c] = y[LINES : 2 * LINES]


def call(kernel, inputs, out_shape, scratch=(), space=VMEM):
    if space is not VMEM:
        inputs = [pltpu.with_memory_space_constraint(x, space) for x in inputs]
        space = pl.BlockSpec(memory_space=space)
    return pl.pallas_call(
        kernel,
        out_shape=out_shape,
        in_specs=[space] * len(inputs),
        out_specs=jax.tree.map(lambda _: VMEM, out_shape),
        scratch_shapes=list(scratch),
        compiler_params=pltpu.CompilerParams(vmem_limit_bytes=VMEM_LIMIT),
    )(*inputs)


def shape(*dims):
    return jax.ShapeDtypeStruct(dims, F32)


def per_device(
    adjoint_rhs, block_inverse, x_couplings, y_couplings, perf_cell, perf_well, perf_weight, well_adjoint
):
    held = well_adjoint.shape[1]
    lines = lax.axis_size("gy")
    perfs = perf_cell.shape[0]

    packed = call(
        pack_kernel,
        [
            adjoint_rhs.reshape(6, LINES, 128),
            block_inverse.reshape(9, LINES, 128),
            x_couplings.reshape(6, LINES, 128),
            y_couplings.reshape(6, LINES, 128),
            perf_cell.reshape(1, perfs),
            perf_well.reshape(1, perfs),
            perf_weight.reshape(1, perfs),
            well_adjoint,
        ],
        shape(PLANES, PAIRS, ZC, 128),
        [
            pltpu.VMEM((6, LINES, 128), F32),
            pltpu.VMEM((9, LINES, 128), F32),
            pltpu.VMEM((6, LINES, 128), F32),
            pltpu.VMEM((6, LINES, 128), F32),
            pltpu.VMEM((1, perfs), jnp.int32),
            pltpu.VMEM((1, perfs), jnp.int32),
            pltpu.VMEM((1, perfs), F32),
            pltpu.VMEM((3, held), F32),
            pltpu.VMEM((ZC, 128), F32),
            pltpu.VMEM((PAIRS, 128, 128), F32),
            pltpu.SemaphoreType.DMA((8,)),
        ],
        space=pltpu.HBM,
    )
    chunks = lax.all_to_all(packed, "gx", 0, 0)

    strip = shape(STRIPS + 2, ZC, 128)
    near, far, wells = call(strip_kernel, [chunks], [strip, strip, shape(lines, PLANES, 128)])
    near = lax.ppermute(near, "gy", [(b, b ^ 1) for b in range(lines)])
    far = lax.ppermute(far, "gy", [(b, ((b + 1) ^ 1) - 1) for b in range(1, lines - 1)])

    wells = lax.all_to_all(wells, "gy", 0, 0)

    back = call(
        functools.partial(march_kernel, lines.bit_length() - 1, held.bit_length() - 1),
        [chunks, wells, near, far],
        shape(PLANES, 7, 8, 128),
        [
            pltpu.VMEM((PLANES, 27, ZC, 128), F32),
            pltpu.VMEM((PLANES, 6, ZC, 128), F32),
            pltpu.VMEM((PLANES, 3, ZC, 128), F32),
        ],
    )
    got = lax.all_to_all(back, "gx", 0, 0)
    sums = jnp.broadcast_to(jnp.sum(got[:, 6], axis=0), (lines, 8, 128))
    sums = lax.all_to_all(sums, "gy", 0, 0)
    precond, well_update = call(
        unpack_kernel,
        [got, sums],
        [shape(2, 3, LINES, 128), shape(3, held)],
        [pltpu.VMEM((3, 128, 128), F32)],
    )
    return precond.reshape(adjoint_rhs.shape), well_update


def solution(mesh):
    placed = (
        P(None, None, "gx", "gy", None),
        P(None, None, "gx", "gy", None),
        P(None, None, "gx", "gy", None),
        P(None, None, "gx", "gy", None),
        P(("gx", "gy")),
        P(("gx", "gy")),
        P(("gx", "gy")),
        P(None, ("gx", "gy")),
    )
    return jax.shard_map(
        per_device,
        mesh=mesh,
        in_specs=placed,
        out_specs=(P(None, None, "gx", "gy", None), P(None, ("gx", "gy"))),
        check_vma=False,
    )
```

```python
import functools

import jax
import jax.numpy as jnp
from jax import lax
from jax.experimental import pallas as pl
from jax.experimental.pallas import tpu as pltpu
from jax.sharding import PartitionSpec as P

F32 = jnp.float32
BF16 = jnp.bfloat16
PLANES = 8
LINES = 64
ZC = 16
PAIRS = 14
WELL_ROW = 3
STRIPS = PLANES * PAIRS // 4
VMEM_LIMIT = 24 * 1024 * 1024

VMEM = pl.BlockSpec(memory_space=pltpu.VMEM)


def split3(x):
    hi = x.astype(BF16).astype(F32)
    rest = x - hi
    mid = rest.astype(BF16).astype(F32)
    lo = rest - mid
    return hi, mid, lo


def split_rows(x):
    return jnp.concatenate(split3(x), axis=0).astype(BF16)


def join_rows(y, rows):
    return y[0:rows] + y[rows : 2 * rows] + y[2 * rows : 3 * rows]


def lane_iota(rows):
    return lax.broadcasted_iota(jnp.int32, (rows, 128), 1)


def row_iota(rows):
    return lax.broadcasted_iota(jnp.int32, (rows, 128), 0)


def roll_lanes(x, shift):
    shift %= 128
    return x if shift == 0 else pltpu.roll(x, shift, 1)


def pack_kernel(rhs, einv, xc, yc, cell, well, weight, wells, *rest):
    out, rhs_v, einv_v, xc_v, yc_v, cell_v, well_v, weight_v, wells_v, wide, turned, sems = rest
    moves = [
        pltpu.make_async_copy(src, dst, sems.at[i])
        for i, (src, dst) in enumerate(
            [
                (rhs, rhs_v),
                (einv, einv_v),
                (xc, xc_v),
                (yc, yc_v),
                (cell, cell_v),
                (well, well_v),
                (weight, weight_v),
                (wells, wells_v),
            ]
        )
    ]
    for move in moves:
        move.start()
    arrays = (
        [(rhs_v, 0, i) for i in range(6)]
        + [(einv_v, 1, i) for i in range(9)]
        + [(xc_v, 2, i) for i in range(6)]
        + [(yc_v, 3, i) for i in range(6)]
    )
    waited = -1
    for g in range(PAIRS):
        ends = []
        for n in (2 * g, 2 * g + 1):
            if n == 27:
                ends.append(jnp.zeros((LINES, 128), F32))
                continue
            ref, stage, i = arrays[n]
            if stage > waited:
                moves[stage].wait()
                waited = stage
            ends.append(ref[i])
        turned[g] = jnp.concatenate(ends, axis=0).T
    for stage in (4, 5, 6, 7):
        moves[stage].wait()
    held = wells_v.shape[1]
    wide[...] = jnp.zeros_like(wide)
    wide[0, 0:LINES] = cell_v[0].astype(F32)
    wide[1, 0:LINES] = well_v[0].astype(F32)
    wide[2, 0:LINES] = weight_v[0]
    wide[8:11, 0:held] = wells_v[...]
    own = wide[8:9] + roll_lanes(wide[9:10], held) + roll_lanes(wide[10:11], 2 * held)
    wide[8:11] = jnp.zeros((3, 128), F32)
    wide[WELL_ROW : WELL_ROW + 1] = own
    perfs = roll_lanes(wide[...], 64)
    low = lane_iota(ZC) < 64
    for t in range(PLANES):
        rows = slice(ZC * t, ZC * t + ZC)
        for g in range(PAIRS - 1):
            out[t, g] = turned[g, rows, :]
        out[t, PAIRS - 1] = jnp.where(low, turned[PAIRS - 1, rows, :], perfs)


def perf_tiles(chunks):
    low = lane_iota(8) < 64
    last = PAIRS - 1
    return [
        jnp.where(low, roll_lanes(chunks[2 * j, last, 0:8], 64), chunks[2 * j + 1, last, 0:8])
        for j in range(PLANES // 2)
    ]


def ints(row):
    return row.astype(jnp.int32)


def place_of(tile, first_z):
    cell = ints(tile[0:1])
    at_z = (cell & 127) == row_iota(ZC) + first_z
    at_y = jnp.where(((cell >> 7) & 63) == row_iota(128), 1.0, 0.0).astype(BF16)
    return at_z, at_y


def sides(at_z):
    low = lane_iota(ZC) < 64
    return [jnp.logical_and(at_z, low), jnp.logical_and(at_z, jnp.logical_not(low))]


def strip_kernel(chunks, near_ref, far_ref, wells_ref):
    last = PAIRS - 1
    own = jnp.concatenate([chunks[d, last, WELL_ROW : WELL_ROW + 1] for d in range(PLANES)], axis=0)
    wells_ref[...] = jnp.broadcast_to(roll_lanes(own, 64)[None], wells_ref.shape)
    tiles = perf_tiles(chunks)
    for u in range(2):
        pair = jnp.concatenate([tiles[2 * u], tiles[2 * u + 1]], axis=0)
        near_ref[STRIPS + u] = pair
        far_ref[STRIPS + u] = pair
    lane = lane_iota(ZC)
    odd = lax.axis_index("gy") & 1
    near_slot = ((lane - 48 * (1 - odd)) & 63) >> 4
    far_slot = ((lane - 48 * odd) & 63) >> 4
    for q in range(STRIPS):
        near = far = None
        for s in range(4):
            d, g = divmod(4 * q + s, PAIRS)
            x = roll_lanes(chunks[d, g], 16 * s)
            near = x if s == 0 else jnp.where(near_slot == s, x, near)
            far = x if s == 0 else jnp.where(far_slot == s, x, far)
        near_ref[q] = near
        far_ref[q] = far


def block_apply(blocks, v):
    return [blocks[3 * a] * v[0] + blocks[3 * a + 1] * v[1] + blocks[3 * a + 2] * v[2] for a in range(3)]


def plane_apply(blocks, lower, upper, v):
    w = block_apply(blocks, v)
    u = [v[c] - lower[c] * roll_lanes(w[c], 1) - upper[c] * roll_lanes(w[c], 127) for c in range(3)]
    return block_apply(blocks, u)


def sources(line_bits, bits, chunks, wells_ref, near, far, src):
    held = 1 << bits
    first_z = lax.axis_index("gx") * ZC
    wells = split_rows(wells_ref[...].reshape(-1, 128).T[0:ZC])
    own = perf_tiles(chunks)
    row = row_iota(128)
    odd = lax.axis_index("gy") & 1
    start = [64 + 48 * odd, 112 - 48 * odd]
    spans = [row < 64] + [jnp.logical_and(row >= first, row < first + 16) for first in start]
    for j in range(PLANES // 2):
        half = slice(8 * (j % 2), 8 * (j % 2) + 8)
        total = None
        for tile, span, base in zip([own[j], near[STRIPS + j // 2, half], far[STRIPS + j // 2, half]], spans, (0, 64, 64)):
            well = ints(tile[1:2])
            owner = well >> bits
            at = (owner & ((1 << line_bits) - 1)) * PLANES + (owner >> line_bits)
            hot = jnp.where(at == row_iota(wells.shape[1]), 1.0, 0.0).astype(BF16)
            picked = join_rows(jnp.dot(wells, hot, preferred_element_type=F32), ZC)
            terms = []
            for c in range(3):
                term = jnp.zeros((1, 128), F32)
                for i in range(held):
                    term = jnp.where((well & (held - 1)) == i, picked[held * c + i : held * c + i + 1], term)
                terms.append(term * tile[2:3])
            cell = ints(tile[0:1])
            at_z = (cell & 127) == row_iota(ZC) + first_z
            at_y = ((cell >> 7) & 63) + base == row
            at_y = jnp.where(jnp.logical_and(at_y, span), 1.0, 0.0).astype(BF16)
            rows = [jnp.where(keep, term, 0.0) for keep in sides(at_z) for term in terms]
            rows = split_rows(jnp.concatenate(rows, axis=0))
            spread = lax.dot_general(rows, at_y, (((1,), (1,)), ((), ())), preferred_element_type=F32)
            total = spread if total is None else total + spread
        total = join_rows(total, 6 * ZC)
        for side in range(2):
            for c in range(3):
                src[2 * j + side, c] = total[(3 * side + c) * ZC : (3 * side + c + 1) * ZC]


def march_kernel(line_bits, bits, chunks, wells_ref, near, far, out_ref, grid, field, src):
    share = line_bits + bits
    me = lax.axis_index("gx")
    sources(line_bits, bits, chunks, wells_ref, near, far, src)
    lane = lane_iota(ZC)
    own = lane < 64
    odd = lax.axis_index("gy") & 1
    slot = lane >> 4
    outside = jnp.logical_or(lane < 80, lane >= 112)

    for d in range(PLANES):
        for g in range(PAIRS):
            q, s = divmod(PAIRS * d + g, 4)
            x = chunks[d, g]
            ends = (near[q], far[q])
            for h in range(2):
                n = 2 * g + h
                if n == 27:
                    continue
                at = 16 * s + 64 * h
                first = at // 16
                edge = jnp.where(slot == ((first + 3 * odd) & 7), *ends)
                edge = jnp.where(outside, roll_lanes(edge, 64 - at), 0.0)
                value = jnp.where(own, roll_lanes(x, 64 * h), edge)
                if n < 6:
                    value = value + src[d, n % 3]
                grid[d, n] = value

    tiles = perf_tiles(chunks)
    row = row_iota(128)
    places = [place_of(tile, me * ZC) for tile in tiles]
    found = [None] * (PLANES // 2)

    def finish(i, planes):
        for c in range(3):
            pair = jnp.where(own, planes[0][c], roll_lanes(planes[1][c], 64))
            out_ref[i, 2 * c] = pair[0:8]
            out_ref[i, 2 * c + 1] = pair[8:16]
        at_z, at_y = places[i // 2]
        x = split_rows(jnp.concatenate(planes[1], axis=0))
        got = join_rows(jnp.dot(x, at_y, preferred_element_type=F32), 48)
        keep = sides(at_z)[i % 2]
        got = [jnp.where(keep, got[16 * c : 16 * c + 16], 0.0) for c in range(3)]
        sofar = found[i // 2]
        found[i // 2] = got if sofar is None else [a + b for a, b in zip(sofar, got)]

    state = None
    for i in range(PLANES):
        blocks = [grid[i, 6 + n] for n in range(9)]
        lower = [grid[i, 21 + c] for c in range(3)]
        upper = [grid[i, 24 + c] for c in range(3)]
        new = []
        for k in range(2):
            v = [grid[i, 3 * k + c] for c in range(3)]
            if i > 0:
                v = [v[c] - grid[i, 15 + c] * state[k][c] for c in range(3)]
            new.append(plane_apply(blocks, lower, upper, v))
        state = new
        if i < PLANES - 1:
            for k in range(2):
                for c in range(3):
                    field[i, 3 * k + c] = state[k][c]
    finish(PLANES - 1, state)
    for i in range(PLANES - 2, -1, -1):
        blocks = [grid[i, 6 + n] for n in range(9)]
        lower = [grid[i, 21 + c] for c in range(3)]
        upper = [grid[i, 24 + c] for c in range(3)]
        new = []
        for k in range(2):
            v = [grid[i, 18 + c] * state[k][c] for c in range(3)]
            p = plane_apply(blocks, lower, upper, v)
            new.append([field[i, 3 * k + c] - p[c] for c in range(3)])
        state = new
        finish(i, state)

    total = None
    for j in range(PLANES // 2):
        well = ints(tiles[j][1:2])
        value = [jnp.sum(f, axis=0, keepdims=True) * tiles[j][2:3] for f in found[j]]
        rows = [jnp.where((well >> share) == i, v, 0.0) for i in range(PLANES) for v in value]
        rows = jnp.concatenate(list(split3(jnp.concatenate(rows, axis=0))) + [jnp.zeros((8, 128), F32)], axis=0)
        hot = jnp.where((well & ((1 << share) - 1)) == row, 1.0, 0.0).astype(BF16)
        part = lax.dot_general(rows.astype(BF16), hot, (((1,), (1,)), ((), ())), preferred_element_type=F32)
        total = part if total is None else total + part
    total = join_rows(total, 3 * PLANES)
    for i in range(PLANES):
        out_ref[i, 6] = jnp.concatenate([total[3 * i : 3 * i + 3], jnp.zeros((5, 128), F32)], axis=0)


def unpack_kernel(chunks, sums, out, wells, turned):
    held = wells.shape[1]
    total = sums[0]
    for b in range(1, sums.shape[0]):
        total = total + sums[b]
    shift = (128 - held * lax.axis_index("gy")) & 127
    wells[...] = pltpu.roll(total, shift, 1)[0:3, 0:held]
    for t in range(PLANES):
        for c in range(3):
            for h in range(2):
                turned[c, ZC * t + 8 * h : ZC * t + 8 * h + 8] = chunks[t, 2 * c + h]
    for c in range(3):
        y = turned[c].T
        out[0, c] = y[0:LINES]
        out[1, c] = y[LINES : 2 * LINES]


def call(kernel, inputs, out_shape, scratch=(), space=VMEM):
    if space is not VMEM:
        inputs = [pltpu.with_memory_space_constraint(x, space) for x in inputs]
        space = pl.BlockSpec(memory_space=space)
    return pl.pallas_call(
        kernel,
        out_shape=out_shape,
        in_specs=[space] * len(inputs),
        out_specs=jax.tree.map(lambda _: VMEM, out_shape),
        scratch_shapes=list(scratch),
        compiler_params=pltpu.CompilerParams(vmem_limit_bytes=VMEM_LIMIT),
    )(*inputs)


def shape(*dims):
    return jax.ShapeDtypeStruct(dims, F32)


def per_device(
    adjoint_rhs, block_inverse, x_couplings, y_couplings, perf_cell, perf_well, perf_weight, well_adjoint
):
    held = well_adjoint.shape[1]
    lines = lax.axis_size("gy")
    perfs = perf_cell.shape[0]

    packed = call(
        pack_kernel,
        [
            adjoint_rhs.reshape(6, LINES, 128),
            block_inverse.reshape(9, LINES, 128),
            x_couplings.reshape(6, LINES, 128),
            y_couplings.reshape(6, LINES, 128),
            perf_cell.reshape(1, perfs),
            perf_well.reshape(1, perfs),
            perf_weight.reshape(1, perfs),
            well_adjoint,
        ],
        shape(PLANES, PAIRS, ZC, 128),
        [
            pltpu.VMEM((6, LINES, 128), F32),
            pltpu.VMEM((9, LINES, 128), F32),
            pltpu.VMEM((6, LINES, 128), F32),
            pltpu.VMEM((6, LINES, 128), F32),
            pltpu.VMEM((1, perfs), jnp.int32),
            pltpu.VMEM((1, perfs), jnp.int32),
            pltpu.VMEM((1, perfs), F32),
            pltpu.VMEM((3, held), F32),
            pltpu.VMEM((ZC, 128), F32),
            pltpu.VMEM((PAIRS, 128, 128), F32),
            pltpu.SemaphoreType.DMA((8,)),
        ],
        space=pltpu.HBM,
    )
    chunks = lax.all_to_all(packed, "gx", 0, 0)

    strip = shape(STRIPS + 2, ZC, 128)
    near, far, wells = call(strip_kernel, [chunks], [strip, strip, shape(lines, PLANES, 128)])
    near = lax.ppermute(near, "gy", [(b, b ^ 1) for b in range(lines)])
    far = lax.ppermute(far, "gy", [(b, ((b + 1) ^ 1) - 1) for b in range(1, lines - 1)])

    wells = lax.all_to_all(wells, "gy", 0, 0)

    back = call(
        functools.partial(march_kernel, lines.bit_length() - 1, held.bit_length() - 1),
        [chunks, wells, near, far],
        shape(PLANES, 7, 8, 128),
        [
            pltpu.VMEM((PLANES, 27, ZC, 128), F32),
            pltpu.VMEM((PLANES, 6, ZC, 128), F32),
            pltpu.VMEM((PLANES, 3, ZC, 128), F32),
        ],
    )
    got = lax.all_to_all(back, "gx", 0, 0)
    sums = jnp.broadcast_to(jnp.sum(got[:, 6], axis=0), (lines, 8, 128))
    sums = lax.all_to_all(sums, "gy", 0, 0)
    precond, well_update = call(
        unpack_kernel,
        [got, sums],
        [shape(2, 3, LINES, 128), shape(3, held)],
        [pltpu.VMEM((3, 128, 128), F32)],
    )
    return precond.reshape(adjoint_rhs.shape), well_update


def solution(mesh):
    placed = (
        P(None, None, "gx", "gy", None),
        P(None, None, "gx", "gy", None),
        P(None, None, "gx", "gy", None),
        P(None, None, "gx", "gy", None),
        P(("gx", "gy")),
        P(("gx", "gy")),
        P(("gx", "gy")),
        P(None, ("gx", "gy")),
    )
    return jax.shard_map(
        per_device,
        mesh=mesh,
        in_specs=placed,
        out_specs=(P(None, None, "gx", "gy", None), P(None, ("gx", "gy"))),
        check_vma=False,
    )
```

```python
import functools

import jax
import jax.numpy as jnp
from jax import lax
from jax.experimental import pallas as pl
from jax.experimental.pallas import tpu as pltpu
from jax.sharding import PartitionSpec as P

F32 = jnp.float32
BF16 = jnp.bfloat16
PLANES = 8
LINES = 64
ZC = 16
PAIRS = 14
WELL_ROW = 3
STRIPS = PLANES * PAIRS // 4
VMEM_LIMIT = 24 * 1024 * 1024

VMEM = pl.BlockSpec(memory_space=pltpu.VMEM)


def split3(x):
    hi = x.astype(BF16).astype(F32)
    rest = x - hi
    mid = rest.astype(BF16).astype(F32)
    lo = rest - mid
    return hi, mid, lo


def split_rows(x):
    return jnp.concatenate(split3(x), axis=0).astype(BF16)


def join_rows(y, rows):
    return y[0:rows] + y[rows : 2 * rows] + y[2 * rows : 3 * rows]


def lane_iota(rows):
    return lax.broadcasted_iota(jnp.int32, (rows, 128), 1)


def row_iota(rows):
    return lax.broadcasted_iota(jnp.int32, (rows, 128), 0)


def roll_lanes(x, shift):
    shift %= 128
    return x if shift == 0 else pltpu.roll(x, shift, 1)


def pack_kernel(rhs, einv, xc, yc, cell, well, weight, wells, *rest):
    out, rhs_v, einv_v, xc_v, yc_v, cell_v, well_v, weight_v, wells_v, wide, turned, sems = rest
    moves = [
        pltpu.make_async_copy(src, dst, sems.at[i])
        for i, (src, dst) in enumerate(
            [
                (rhs, rhs_v),
                (einv, einv_v),
                (xc, xc_v),
                (yc, yc_v),
                (cell, cell_v),
                (well, well_v),
                (weight, weight_v),
                (wells, wells_v),
            ]
        )
    ]
    for move in moves:
        move.start()
    arrays = (
        [(rhs_v, 0, i) for i in range(6)]
        + [(einv_v, 1, i) for i in range(9)]
        + [(xc_v, 2, i) for i in range(6)]
        + [(yc_v, 3, i) for i in range(6)]
    )
    waited = -1
    for g in range(PAIRS):
        ends = []
        for n in (2 * g, 2 * g + 1):
            if n == 27:
                ends.append(jnp.zeros((LINES, 128), F32))
                continue
            ref, stage, i = arrays[n]
            if stage > waited:
                moves[stage].wait()
                waited = stage
            ends.append(ref[i])
        turned[g] = jnp.concatenate(ends, axis=0).T
    for stage in (4, 5, 6, 7):
        moves[stage].wait()
    held = wells_v.shape[1]
    wide[...] = jnp.zeros_like(wide)
    wide[0, 0:LINES] = cell_v[0].astype(F32)
    wide[1, 0:LINES] = well_v[0].astype(F32)
    wide[2, 0:LINES] = weight_v[0]
    wide[8:11, 0:held] = wells_v[...]
    own = wide[8:9] + roll_lanes(wide[9:10], held) + roll_lanes(wide[10:11], 2 * held)
    wide[8:11] = jnp.zeros((3, 128), F32)
    wide[WELL_ROW : WELL_ROW + 1] = own
    perfs = roll_lanes(wide[...], 64)
    low = lane_iota(ZC) < 64
    for t in range(PLANES):
        rows = slice(ZC * t, ZC * t + ZC)
        for g in range(PAIRS - 1):
            out[t, g] = turned[g, rows, :]
        out[t, PAIRS - 1] = jnp.where(low, turned[PAIRS - 1, rows, :], perfs)


def perf_tiles(chunks):
    low = lane_iota(8) < 64
    last = PAIRS - 1
    return [
        jnp.where(low, roll_lanes(chunks[2 * j, last, 0:8], 64), chunks[2 * j + 1, last, 0:8])
        for j in range(PLANES // 2)
    ]


def ints(row):
    return row.astype(jnp.int32)


def place_of(tile, first_z):
    cell = ints(tile[0:1])
    at_z = (cell & 127) == row_iota(ZC) + first_z
    at_y = jnp.where(((cell >> 7) & 63) == row_iota(128), 1.0, 0.0).astype(BF16)
    return at_z, at_y


def sides(at_z):
    low = lane_iota(ZC) < 64
    return [jnp.logical_and(at_z, low), jnp.logical_and(at_z, jnp.logical_not(low))]


def strip_kernel(chunks, near_ref, far_ref, wells_ref):
    own = jnp.zeros((1, 128), F32)
    held_lanes = (lane_iota(1) >> 4) == 4
    for d in range(PLANES):
        row = jnp.where(held_lanes, chunks[d, PAIRS - 1, WELL_ROW : WELL_ROW + 1], 0.0)
        own = own + roll_lanes(row, 64 + ZC * d)
    wells_ref[...] = jnp.broadcast_to(own, wells_ref.shape)
    tiles = perf_tiles(chunks)
    for u in range(2):
        pair = jnp.concatenate([tiles[2 * u], tiles[2 * u + 1]], axis=0)
        near_ref[STRIPS + u] = pair
        far_ref[STRIPS + u] = pair
    lane = lane_iota(ZC)
    odd = lax.axis_index("gy") & 1
    near_slot = ((lane - 48 * (1 - odd)) & 63) >> 4
    far_slot = ((lane - 48 * odd) & 63) >> 4
    for q in range(STRIPS):
        near = far = None
        for s in range(4):
            d, g = divmod(4 * q + s, PAIRS)
            x = roll_lanes(chunks[d, g], 16 * s)
            near = x if s == 0 else jnp.where(near_slot == s, x, near)
            far = x if s == 0 else jnp.where(far_slot == s, x, far)
        near_ref[q] = near
        far_ref[q] = far


def block_apply(blocks, v):
    return [blocks[3 * a] * v[0] + blocks[3 * a + 1] * v[1] + blocks[3 * a + 2] * v[2] for a in range(3)]


def plane_apply(blocks, lower, upper, v):
    w = block_apply(blocks, v)
    u = [v[c] - lower[c] * roll_lanes(w[c], 1) - upper[c] * roll_lanes(w[c], 127) for c in range(3)]
    return block_apply(blocks, u)


def sources(line_bits, bits, chunks, wells_ref, near, far, src):
    held = 1 << bits
    first_z = lax.axis_index("gx") * ZC
    rows = wells_ref[...]
    turned = jnp.concatenate([rows, jnp.zeros((128 - rows.shape[0], 128), F32)], axis=0).T
    quarter = lane_iota(ZC) >> 5
    wells = []
    for u in range(2):
        tile = None
        for v in range(4):
            d = 4 * u + v
            part = roll_lanes(turned[ZC * d : ZC * d + ZC], 32 * v)
            tile = part if v == 0 else jnp.where(quarter == v, part, tile)
        wells.append(tile)
    wells = split_rows(jnp.concatenate(wells, axis=1))
    own = perf_tiles(chunks)
    row = row_iota(128)
    odd = lax.axis_index("gy") & 1
    start = [64 + 48 * odd, 112 - 48 * odd]
    spans = [row < 64] + [jnp.logical_and(row >= first, row < first + 16) for first in start]
    for j in range(PLANES // 2):
        half = slice(8 * (j % 2), 8 * (j % 2) + 8)
        total = None
        for tile, span, base in zip([own[j], near[STRIPS + j // 2, half], far[STRIPS + j // 2, half]], spans, (0, 64, 64)):
            well = ints(tile[1:2])
            owner = well >> bits
            at = (owner >> line_bits) * 32 + (owner & ((1 << line_bits) - 1))
            hot = jnp.where(at == row_iota(wells.shape[1]), 1.0, 0.0).astype(BF16)
            picked = join_rows(jnp.dot(wells, hot, preferred_element_type=F32), ZC)
            terms = []
            for c in range(3):
                term = jnp.zeros((1, 128), F32)
                for i in range(held):
                    term = jnp.where((well & (held - 1)) == i, picked[held * c + i : held * c + i + 1], term)
                terms.append(term * tile[2:3])
            cell = ints(tile[0:1])
            at_z = (cell & 127) == row_iota(ZC) + first_z
            at_y = ((cell >> 7) & 63) + base == row
            at_y = jnp.where(jnp.logical_and(at_y, span), 1.0, 0.0).astype(BF16)
            rows = [jnp.where(keep, term, 0.0) for keep in sides(at_z) for term in terms]
            rows = split_rows(jnp.concatenate(rows, axis=0))
            spread = lax.dot_general(rows, at_y, (((1,), (1,)), ((), ())), preferred_element_type=F32)
            total = spread if total is None else total + spread
        total = join_rows(total, 6 * ZC)
        for side in range(2):
            for c in range(3):
                src[2 * j + side, c] = total[(3 * side + c) * ZC : (3 * side + c + 1) * ZC]


def march_kernel(line_bits, bits, chunks, wells_ref, near, far, out_ref, grid, field, src):
    share = line_bits + bits
    me = lax.axis_index("gx")
    sources(line_bits, bits, chunks, wells_ref, near, far, src)
    lane = lane_iota(ZC)
    own = lane < 64
    odd = lax.axis_index("gy") & 1
    slot = lane >> 4
    outside = jnp.logical_or(lane < 80, lane >= 112)

    for d in range(PLANES):
        for g in range(PAIRS):
            q, s = divmod(PAIRS * d + g, 4)
            x = chunks[d, g]
            ends = (near[q], far[q])
            for h in range(2):
                n = 2 * g + h
                if n == 27:
                    continue
                at = 16 * s + 64 * h
                first = at // 16
                edge = jnp.where(slot == ((first + 3 * odd) & 7), *ends)
                edge = jnp.where(outside, roll_lanes(edge, 64 - at), 0.0)
                value = jnp.where(own, roll_lanes(x, 64 * h), edge)
                if n < 6:
                    value = value + src[d, n % 3]
                grid[d, n] = value

    tiles = perf_tiles(chunks)
    row = row_iota(128)
    places = [place_of(tile, me * ZC) for tile in tiles]
    found = [None] * (PLANES // 2)

    def finish(i, planes):
        for c in range(3):
            pair = jnp.where(own, planes[0][c], roll_lanes(planes[1][c], 64))
            out_ref[i, 2 * c] = pair[0:8]
            out_ref[i, 2 * c + 1] = pair[8:16]
        at_z, at_y = places[i // 2]
        x = split_rows(jnp.concatenate(planes[1], axis=0))
        got = join_rows(jnp.dot(x, at_y, preferred_element_type=F32), 48)
        keep = sides(at_z)[i % 2]
        got = [jnp.where(keep, got[16 * c : 16 * c + 16], 0.0) for c in range(3)]
        sofar = found[i // 2]
        found[i // 2] = got if sofar is None else [a + b for a, b in zip(sofar, got)]

    state = None
    for i in range(PLANES):
        blocks = [grid[i, 6 + n] for n in range(9)]
        lower = [grid[i, 21 + c] for c in range(3)]
        upper = [grid[i, 24 + c] for c in range(3)]
        new = []
        for k in range(2):
            v = [grid[i, 3 * k + c] for c in range(3)]
            if i > 0:
                v = [v[c] - grid[i, 15 + c] * state[k][c] for c in range(3)]
            new.append(plane_apply(blocks, lower, upper, v))
        state = new
        if i < PLANES - 1:
            for k in range(2):
                for c in range(3):
                    field[i, 3 * k + c] = state[k][c]
    finish(PLANES - 1, state)
    for i in range(PLANES - 2, -1, -1):
        blocks = [grid[i, 6 + n] for n in range(9)]
        lower = [grid[i, 21 + c] for c in range(3)]
        upper = [grid[i, 24 + c] for c in range(3)]
        new = []
        for k in range(2):
            v = [grid[i, 18 + c] * state[k][c] for c in range(3)]
            p = plane_apply(blocks, lower, upper, v)
            new.append([field[i, 3 * k + c] - p[c] for c in range(3)])
        state = new
        finish(i, state)

    total = None
    for j in range(PLANES // 2):
        well = ints(tiles[j][1:2])
        value = [jnp.sum(f, axis=0, keepdims=True) * tiles[j][2:3] for f in found[j]]
        rows = [jnp.where((well >> share) == i, v, 0.0) for i in range(PLANES) for v in value]
        rows = jnp.concatenate(list(split3(jnp.concatenate(rows, axis=0))) + [jnp.zeros((8, 128), F32)], axis=0)
        hot = jnp.where((well & ((1 << share) - 1)) == row, 1.0, 0.0).astype(BF16)
        part = lax.dot_general(rows.astype(BF16), hot, (((1,), (1,)), ((), ())), preferred_element_type=F32)
        total = part if total is None else total + part
    total = join_rows(total, 3 * PLANES)
    for i in range(PLANES):
        out_ref[i, 6] = jnp.concatenate([total[3 * i : 3 * i + 3], jnp.zeros((5, 128), F32)], axis=0)


def unpack_kernel(chunks, sums, out, wells, turned):
    held = wells.shape[1]
    total = sums[0]
    for b in range(1, sums.shape[0]):
        total = total + sums[b]
    shift = (128 - held * lax.axis_index("gy")) & 127
    wells[...] = pltpu.roll(total, shift, 1)[0:3, 0:held]
    for t in range(PLANES):
        for c in range(3):
            for h in range(2):
                turned[c, ZC * t + 8 * h : ZC * t + 8 * h + 8] = chunks[t, 2 * c + h]
    for c in range(3):
        y = turned[c].T
        out[0, c] = y[0:LINES]
        out[1, c] = y[LINES : 2 * LINES]


def call(kernel, inputs, out_shape, scratch=(), space=VMEM):
    if space is not VMEM:
        inputs = [pltpu.with_memory_space_constraint(x, space) for x in inputs]
        space = pl.BlockSpec(memory_space=space)
    return pl.pallas_call(
        kernel,
        out_shape=out_shape,
        in_specs=[space] * len(inputs),
        out_specs=jax.tree.map(lambda _: VMEM, out_shape),
        scratch_shapes=list(scratch),
        compiler_params=pltpu.CompilerParams(vmem_limit_bytes=VMEM_LIMIT),
    )(*inputs)


def shape(*dims):
    return jax.ShapeDtypeStruct(dims, F32)


def per_device(
    adjoint_rhs, block_inverse, x_couplings, y_couplings, perf_cell, perf_well, perf_weight, well_adjoint
):
    held = well_adjoint.shape[1]
    lines = lax.axis_size("gy")
    perfs = perf_cell.shape[0]

    packed = call(
        pack_kernel,
        [
            adjoint_rhs.reshape(6, LINES, 128),
            block_inverse.reshape(9, LINES, 128),
            x_couplings.reshape(6, LINES, 128),
            y_couplings.reshape(6, LINES, 128),
            perf_cell.reshape(1, perfs),
            perf_well.reshape(1, perfs),
            perf_weight.reshape(1, perfs),
            well_adjoint,
        ],
        shape(PLANES, PAIRS, ZC, 128),
        [
            pltpu.VMEM((6, LINES, 128), F32),
            pltpu.VMEM((9, LINES, 128), F32),
            pltpu.VMEM((6, LINES, 128), F32),
            pltpu.VMEM((6, LINES, 128), F32),
            pltpu.VMEM((1, perfs), jnp.int32),
            pltpu.VMEM((1, perfs), jnp.int32),
            pltpu.VMEM((1, perfs), F32),
            pltpu.VMEM((3, held), F32),
            pltpu.VMEM((ZC, 128), F32),
            pltpu.VMEM((PAIRS, 128, 128), F32),
            pltpu.SemaphoreType.DMA((8,)),
        ],
        space=pltpu.HBM,
    )
    chunks = lax.all_to_all(packed, "gx", 0, 0)

    strip = shape(STRIPS + 2, ZC, 128)
    near, far, wells = call(strip_kernel, [chunks], [strip, strip, shape(lines, 128)])
    near = lax.ppermute(near, "gy", [(b, b ^ 1) for b in range(lines)])
    far = lax.ppermute(far, "gy", [(b, ((b + 1) ^ 1) - 1) for b in range(1, lines - 1)])

    wells = lax.all_to_all(wells, "gy", 0, 0, tiled=True)

    back = call(
        functools.partial(march_kernel, lines.bit_length() - 1, held.bit_length() - 1),
        [chunks, wells, near, far],
        shape(PLANES, 7, 8, 128),
        [
            pltpu.VMEM((PLANES, 27, ZC, 128), F32),
            pltpu.VMEM((PLANES, 6, ZC, 128), F32),
            pltpu.VMEM((PLANES, 3, ZC, 128), F32),
        ],
    )
    got = lax.all_to_all(back, "gx", 0, 0)
    sums = jnp.broadcast_to(jnp.sum(got[:, 6], axis=0), (lines, 8, 128))
    sums = lax.all_to_all(sums, "gy", 0, 0)
    precond, well_update = call(
        unpack_kernel,
        [got, sums],
        [shape(2, 3, LINES, 128), shape(3, held)],
        [pltpu.VMEM((3, 128, 128), F32)],
    )
    return precond.reshape(adjoint_rhs.shape), well_update


def solution(mesh):
    placed = (
        P(None, None, "gx", "gy", None),
        P(None, None, "gx", "gy", None),
        P(None, None, "gx", "gy", None),
        P(None, None, "gx", "gy", None),
        P(("gx", "gy")),
        P(("gx", "gy")),
        P(("gx", "gy")),
        P(None, ("gx", "gy")),
    )
    return jax.shard_map(
        per_device,
        mesh=mesh,
        in_specs=placed,
        out_specs=(P(None, None, "gx", "gy", None), P(None, ("gx", "gy"))),
        check_vma=False,
    )
```

```python
import functools

import jax
import jax.numpy as jnp
from jax import lax
from jax.experimental import pallas as pl
from jax.experimental.pallas import tpu as pltpu
from jax.sharding import PartitionSpec as P

F32 = jnp.float32
BF16 = jnp.bfloat16
PLANES = 8
LINES = 64
ZC = 16
PAIRS = 14
WELL_ROW = 3
STRIPS = PLANES * PAIRS // 4
VMEM_LIMIT = 24 * 1024 * 1024

VMEM = pl.BlockSpec(memory_space=pltpu.VMEM)


def split3(x):
    hi = x.astype(BF16).astype(F32)
    rest = x - hi
    mid = rest.astype(BF16).astype(F32)
    lo = rest - mid
    return hi, mid, lo


def split_rows(x):
    return jnp.concatenate(split3(x), axis=0).astype(BF16)


def join_rows(y, rows):
    return y[0:rows] + y[rows : 2 * rows] + y[2 * rows : 3 * rows]


def lane_iota(rows):
    return lax.broadcasted_iota(jnp.int32, (rows, 128), 1)


def row_iota(rows):
    return lax.broadcasted_iota(jnp.int32, (rows, 128), 0)


def roll_lanes(x, shift):
    shift %= 128
    return x if shift == 0 else pltpu.roll(x, shift, 1)


def pack_kernel(rhs, einv, xc, yc, cell, well, weight, wells, *rest):
    out, rhs_v, einv_v, xc_v, yc_v, cell_v, well_v, weight_v, wells_v, wide, turned, sems = rest
    moves = [
        pltpu.make_async_copy(src, dst, sems.at[i])
        for i, (src, dst) in enumerate(
            [
                (rhs, rhs_v),
                (einv, einv_v),
                (xc, xc_v),
                (yc, yc_v),
                (cell, cell_v),
                (well, well_v),
                (weight, weight_v),
                (wells, wells_v),
            ]
        )
    ]
    for move in moves:
        move.start()
    arrays = (
        [(rhs_v, 0, i) for i in range(6)]
        + [(einv_v, 1, i) for i in range(9)]
        + [(xc_v, 2, i) for i in range(6)]
        + [(yc_v, 3, i) for i in range(6)]
    )
    waited = -1
    for g in range(PAIRS):
        ends = []
        for n in (2 * g, 2 * g + 1):
            if n == 27:
                ends.append(jnp.zeros((LINES, 128), F32))
                continue
            ref, stage, i = arrays[n]
            if stage > waited:
                moves[stage].wait()
                waited = stage
            ends.append(ref[i])
        turned[g] = jnp.concatenate(ends, axis=0).T
    for stage in (4, 5, 6, 7):
        moves[stage].wait()
    held = wells_v.shape[1]
    wide[...] = jnp.zeros_like(wide)
    wide[0, 0:LINES] = cell_v[0].astype(F32)
    wide[1, 0:LINES] = well_v[0].astype(F32)
    wide[2, 0:LINES] = weight_v[0]
    wide[8:11, 0:held] = wells_v[...]
    own = wide[8:9] + roll_lanes(wide[9:10], held) + roll_lanes(wide[10:11], 2 * held)
    wide[8:11] = jnp.zeros((3, 128), F32)
    wide[WELL_ROW : WELL_ROW + 1] = own
    perfs = roll_lanes(wide[...], 64)
    low = lane_iota(ZC) < 64
    for t in range(PLANES):
        rows = slice(ZC * t, ZC * t + ZC)
        for g in range(PAIRS - 1):
            out[t, g] = turned[g, rows, :]
        out[t, PAIRS - 1] = jnp.where(low, turned[PAIRS - 1, rows, :], perfs)


def perf_tiles(chunks):
    low = lane_iota(8) < 64
    last = PAIRS - 1
    return [
        jnp.where(low, roll_lanes(chunks[2 * j, last, 0:8], 64), chunks[2 * j + 1, last, 0:8])
        for j in range(PLANES // 2)
    ]


def ints(row):
    return row.astype(jnp.int32)


def place_of(tile, first_z):
    cell = ints(tile[0:1])
    at_z = (cell & 127) == row_iota(ZC) + first_z
    at_y = jnp.where(((cell >> 7) & 63) == row_iota(128), 1.0, 0.0).astype(BF16)
    return at_z, at_y


def sides(at_z):
    low = lane_iota(ZC) < 64
    return [jnp.logical_and(at_z, low), jnp.logical_and(at_z, jnp.logical_not(low))]


def strip_kernel(chunks, near_ref, far_ref, wells_ref):
    own = jnp.zeros((1, 128), F32)
    held_lanes = (lane_iota(1) >> 4) == 4
    for d in range(PLANES):
        row = jnp.where(held_lanes, chunks[d, PAIRS - 1, WELL_ROW : WELL_ROW + 1], 0.0)
        own = own + roll_lanes(row, 64 + ZC * d)
    wells_ref[...] = jnp.broadcast_to(own, wells_ref.shape)
    tiles = perf_tiles(chunks)
    for u in range(2):
        pair = jnp.concatenate([tiles[2 * u], tiles[2 * u + 1]], axis=0)
        near_ref[STRIPS + u] = pair
        far_ref[STRIPS + u] = pair
    lane = lane_iota(ZC)
    odd = lax.axis_index("gy") & 1
    near_slot = ((lane - 48 * (1 - odd)) & 63) >> 4
    far_slot = ((lane - 48 * odd) & 63) >> 4
    for q in range(STRIPS):
        near = far = None
        for s in range(4):
            d, g = divmod(4 * q + s, PAIRS)
            x = roll_lanes(chunks[d, g], 16 * s)
            near = x if s == 0 else jnp.where(near_slot == s, x, near)
            far = x if s == 0 else jnp.where(far_slot == s, x, far)
        near_ref[q] = near
        far_ref[q] = far


def block_apply(blocks, v):
    return [blocks[3 * a] * v[0] + blocks[3 * a + 1] * v[1] + blocks[3 * a + 2] * v[2] for a in range(3)]


def plane_apply(blocks, lower, upper, v):
    w = block_apply(blocks, v)
    u = [v[c] - lower[c] * roll_lanes(w[c], 1) - upper[c] * roll_lanes(w[c], 127) for c in range(3)]
    return block_apply(blocks, u)


def sources(line_bits, bits, chunks, wells_ref, near, far, src):
    held = 1 << bits
    first_z = lax.axis_index("gx") * ZC
    rows = wells_ref[...]
    turned = jnp.concatenate([rows, jnp.zeros((128 - rows.shape[0], 128), F32)], axis=0).T
    quarter = lane_iota(ZC) >> 5
    wells = []
    for u in range(2):
        tile = None
        for v in range(4):
            d = 4 * u + v
            part = roll_lanes(turned[ZC * d : ZC * d + ZC], 32 * v)
            tile = part if v == 0 else jnp.where(quarter == v, part, tile)
        wells.append(tile)
    wells = split_rows(jnp.concatenate(wells, axis=1))
    own = perf_tiles(chunks)
    row = row_iota(128)
    odd = lax.axis_index("gy") & 1
    start = [64 + 48 * odd, 112 - 48 * odd]
    spans = [row < 64] + [jnp.logical_and(row >= first, row < first + 16) for first in start]
    for j in range(PLANES // 2):
        half = slice(8 * (j % 2), 8 * (j % 2) + 8)
        total = None
        for tile, span, base in zip([own[j], near[STRIPS + j // 2, half], far[STRIPS + j // 2, half]], spans, (0, 64, 64)):
            well = ints(tile[1:2])
            owner = well >> bits
            at = (owner >> line_bits) * 32 + (owner & ((1 << line_bits) - 1))
            hot = jnp.where(at == row_iota(wells.shape[1]), 1.0, 0.0).astype(BF16)
            picked = join_rows(jnp.dot(wells, hot, preferred_element_type=F32), ZC)
            terms = []
            for c in range(3):
                term = jnp.zeros((1, 128), F32)
                for i in range(held):
                    term = jnp.where((well & (held - 1)) == i, picked[held * c + i : held * c + i + 1], term)
                terms.append(term * tile[2:3])
            cell = ints(tile[0:1])
            at_z = (cell & 127) == row_iota(ZC) + first_z
            at_y = ((cell >> 7) & 63) + base == row
            at_y = jnp.where(jnp.logical_and(at_y, span), 1.0, 0.0).astype(BF16)
            rows = [jnp.where(keep, term, 0.0) for keep in sides(at_z) for term in terms]
            rows = split_rows(jnp.concatenate(rows, axis=0))
            spread = lax.dot_general(rows, at_y, (((1,), (1,)), ((), ())), preferred_element_type=F32)
            total = spread if total is None else total + spread
        total = join_rows(total, 6 * ZC)
        for side in range(2):
            for c in range(3):
                src[2 * j + side, c] = total[(3 * side + c) * ZC : (3 * side + c + 1) * ZC]


def march_kernel(line_bits, bits, chunks, wells_ref, near, far, out_ref, grid, field, src):
    share = line_bits + bits
    me = lax.axis_index("gx")
    sources(line_bits, bits, chunks, wells_ref, near, far, src)
    lane = lane_iota(ZC)
    own = lane < 64
    odd = lax.axis_index("gy") & 1
    slot = lane >> 4
    outside = jnp.logical_or(lane < 80, lane >= 112)

    for d in range(PLANES):
        for g in range(PAIRS):
            q, s = divmod(PAIRS * d + g, 4)
            x = chunks[d, g]
            ends = (near[q], far[q])
            for h in range(2):
                n = 2 * g + h
                if n == 27:
                    continue
                at = 16 * s + 64 * h
                first = at // 16
                edge = jnp.where(slot == ((first + 3 * odd) & 7), *ends)
                edge = jnp.where(outside, roll_lanes(edge, 64 - at), 0.0)
                value = jnp.where(own, roll_lanes(x, 64 * h), edge)
                if n < 6:
                    value = value + src[d, n % 3]
                grid[d, n] = value

    tiles = perf_tiles(chunks)
    row = row_iota(128)
    places = [place_of(tile, me * ZC) for tile in tiles]
    found = [None] * (PLANES // 2)

    def finish(i, planes):
        for c in range(3):
            pair = jnp.where(own, planes[0][c], roll_lanes(planes[1][c], 64))
            out_ref[i, 2 * c] = pair[0:8]
            out_ref[i, 2 * c + 1] = pair[8:16]
        at_z, at_y = places[i // 2]
        x = split_rows(jnp.concatenate(planes[1], axis=0))
        got = join_rows(jnp.dot(x, at_y, preferred_element_type=F32), 48)
        keep = sides(at_z)[i % 2]
        got = [jnp.where(keep, got[16 * c : 16 * c + 16], 0.0) for c in range(3)]
        sofar = found[i // 2]
        found[i // 2] = got if sofar is None else [a + b for a, b in zip(sofar, got)]

    state = None
    for i in range(PLANES):
        blocks = [grid[i, 6 + n] for n in range(9)]
        lower = [grid[i, 21 + c] for c in range(3)]
        upper = [grid[i, 24 + c] for c in range(3)]
        new = []
        for k in range(2):
            v = [grid[i, 3 * k + c] for c in range(3)]
            if i > 0:
                v = [v[c] - grid[i, 15 + c] * state[k][c] for c in range(3)]
            new.append(plane_apply(blocks, lower, upper, v))
        state = new
        if i < PLANES - 1:
            for k in range(2):
                for c in range(3):
                    field[i, 3 * k + c] = state[k][c]
    finish(PLANES - 1, state)
    for i in range(PLANES - 2, -1, -1):
        blocks = [grid[i, 6 + n] for n in range(9)]
        lower = [grid[i, 21 + c] for c in range(3)]
        upper = [grid[i, 24 + c] for c in range(3)]
        new = []
        for k in range(2):
            v = [grid[i, 18 + c] * state[k][c] for c in range(3)]
            p = plane_apply(blocks, lower, upper, v)
            new.append([field[i, 3 * k + c] - p[c] for c in range(3)])
        state = new
        finish(i, state)

    total = None
    for j in range(PLANES // 2):
        well = ints(tiles[j][1:2])
        value = [jnp.sum(f, axis=0, keepdims=True) * tiles[j][2:3] for f in found[j]]
        rows = [jnp.where((well >> share) == i, v, 0.0) for i in range(PLANES) for v in value]
        rows = jnp.concatenate(list(split3(jnp.concatenate(rows, axis=0))) + [jnp.zeros((8, 128), F32)], axis=0)
        hot = jnp.where((well & ((1 << share) - 1)) == row, 1.0, 0.0).astype(BF16)
        part = lax.dot_general(rows.astype(BF16), hot, (((1,), (1,)), ((), ())), preferred_element_type=F32)
        total = part if total is None else total + part
    total = join_rows(total, 3 * PLANES)
    for i in range(PLANES):
        out_ref[i, 6] = jnp.concatenate([total[3 * i : 3 * i + 3], jnp.zeros((5, 128), F32)], axis=0)


def unpack_kernel(chunks, sums, out, wells, turned):
    held = wells.shape[1]
    total = sums[0]
    for b in range(1, sums.shape[0]):
        total = total + sums[b]
    shift = (128 - held * lax.axis_index("gy")) & 127
    wells[...] = pltpu.roll(total, shift, 1)[0:3, 0:held]
    for t in range(PLANES):
        for c in range(3):
            for h in range(2):
                turned[c, ZC * t + 8 * h : ZC * t + 8 * h + 8] = chunks[t, 2 * c + h]
    for c in range(3):
        y = turned[c].T
        out[0, c] = y[0:LINES]
        out[1, c] = y[LINES : 2 * LINES]


def call(kernel, inputs, out_shape, scratch=(), space=VMEM):
    if space is not VMEM:
        inputs = [pltpu.with_memory_space_constraint(x, space) for x in inputs]
        space = pl.BlockSpec(memory_space=space)
    return pl.pallas_call(
        kernel,
        out_shape=out_shape,
        in_specs=[space] * len(inputs),
        out_specs=jax.tree.map(lambda _: VMEM, out_shape),
        scratch_shapes=list(scratch),
        compiler_params=pltpu.CompilerParams(vmem_limit_bytes=VMEM_LIMIT),
    )(*inputs)


def shape(*dims):
    return jax.ShapeDtypeStruct(dims, F32)


def per_device(
    adjoint_rhs, block_inverse, x_couplings, y_couplings, perf_cell, perf_well, perf_weight, well_adjoint
):
    held = well_adjoint.shape[1]
    lines = lax.axis_size("gy")
    perfs = perf_cell.shape[0]

    packed = call(
        pack_kernel,
        [
            adjoint_rhs.reshape(6, LINES, 128),
            block_inverse.reshape(9, LINES, 128),
            x_couplings.reshape(6, LINES, 128),
            y_couplings.reshape(6, LINES, 128),
            perf_cell.reshape(1, perfs),
            perf_well.reshape(1, perfs),
            perf_weight.reshape(1, perfs),
            well_adjoint,
        ],
        shape(PLANES, PAIRS, ZC, 128),
        [
            pltpu.VMEM((6, LINES, 128), F32),
            pltpu.VMEM((9, LINES, 128), F32),
            pltpu.VMEM((6, LINES, 128), F32),
            pltpu.VMEM((6, LINES, 128), F32),
            pltpu.VMEM((1, perfs), jnp.int32),
            pltpu.VMEM((1, perfs), jnp.int32),
            pltpu.VMEM((1, perfs), F32),
            pltpu.VMEM((3, held), F32),
            pltpu.VMEM((ZC, 128), F32),
            pltpu.VMEM((PAIRS, 128, 128), F32),
            pltpu.SemaphoreType.DMA((8,)),
        ],
        space=pltpu.HBM,
    )
    chunks = lax.all_to_all(packed, "gx", 0, 0)

    strip = shape(STRIPS + 2, ZC, 128)
    near, far, wells = call(strip_kernel, [chunks], [strip, strip, shape(lines, 128)])
    near = lax.ppermute(near, "gy", [(b, b ^ 1) for b in range(lines)])
    far = lax.ppermute(far, "gy", [(b, ((b + 1) ^ 1) - 1) for b in range(1, lines - 1)])

    wells = lax.all_to_all(wells, "gy", 0, 0, tiled=True)

    back = call(
        functools.partial(march_kernel, lines.bit_length() - 1, held.bit_length() - 1),
        [chunks, wells, near, far],
        shape(PLANES, 7, 8, 128),
        [
            pltpu.VMEM((PLANES, 27, ZC, 128), F32),
            pltpu.VMEM((PLANES, 6, ZC, 128), F32),
            pltpu.VMEM((PLANES, 3, ZC, 128), F32),
        ],
    )
    got = lax.all_to_all(back, "gx", 0, 0)
    sums = jnp.broadcast_to(jnp.sum(got[:, 6, 0:4], axis=0), (lines, 4, 128))
    sums = lax.all_to_all(sums, "gy", 0, 0)
    precond, well_update = call(
        unpack_kernel,
        [got, sums],
        [shape(2, 3, LINES, 128), shape(3, held)],
        [pltpu.VMEM((3, 128, 128), F32)],
    )
    return precond.reshape(adjoint_rhs.shape), well_update


def solution(mesh):
    placed = (
        P(None, None, "gx", "gy", None),
        P(None, None, "gx", "gy", None),
        P(None, None, "gx", "gy", None),
        P(None, None, "gx", "gy", None),
        P(("gx", "gy")),
        P(("gx", "gy")),
        P(("gx", "gy")),
        P(None, ("gx", "gy")),
    )
    return jax.shard_map(
        per_device,
        mesh=mesh,
        in_specs=placed,
        out_specs=(P(None, None, "gx", "gy", None), P(None, ("gx", "gy"))),
        check_vma=False,
    )
```
